128 devices in a mesh: patch: 16 (over y, z), batch: 8 (over x, core).
Axes of the slice: x: 4, y: 4, z: 4, core: 2. Of those that a mesh axis runs over, the one named last changes fastest.
Arguments:
- latent: bfloat16 [256, 256, 640], P(('batch', 'patch')), parts along dimension 0, may hold values from -12 to 12
- stale_kv: bfloat16 [65536, 1280], P(('batch', 'patch')), parts along dimension 0, may hold values from -100 to 100
- row_counts: int32 [128], P('batch'), parts along dimension 0, may hold values from 1 to 2, 20 in all
- window: int32 [128, 16], P('batch'), parts along dimension 0, may hold values from 0 to 1, as said below
- time_index: int32 [8], P('batch'), parts along dimension 0, may hold values from 0 to 999
- norm_gain: bfloat16 [640], replicated, may hold values from 0.25 to 1.75
- conv_weight: bfloat16 [3, 3, 640, 640], replicated, may hold values from -0.078125 to 0.078125
- time_first: bfloat16 [320, 1280], replicated, may hold values from -0.3125 to 0.3125
- time_second: bfloat16 [1280, 640], replicated, may hold values from -0.15625 to 0.15625
- attn_gain: bfloat16 [640], replicated, may hold values from 0.25 to 1.75
- attn_in: bfloat16 [640, 1920], replicated, may hold values from -0.25 to 0.25
- attn_out: bfloat16 [640, 640], replicated, may hold values from -0.25 to 0.25
Outputs:
- mixed: bfloat16 [256, 256, 640], P(('batch', 'patch')), parts along dimension 0
The draws below stay inside these ranges and needn't reach their ends.
There are 8 independent parts, one for each index of `batch`. The reference program is written for one: setup_inputs(seed, part) draws one part's arguments, and reference() takes and returns one part's arrays. A program takes and returns all parts, laid end to end along the dimension named above; an argument that names none is the same for every part. Nothing has to cross between parts.
Inputs may be any that keep to these rules, and one draw needn't show every extreme that they name: window[p, p] = 1; window[p, j] = 0 where |p - j| > 8. `row_counts`: the counts sum to 20.
All inputs are finite; a program needn't handle non-finite values.
Results may differ from the reference program's by a relative error of at most 0.028.
Values may be sent and summed in bfloat16 or wider, within the bound.
A program may use at most 192 MiB of HBM per device.

```python
import math
import jax
import jax.numpy as jnp
import numpy as np
from jax import lax

CHANNELS = 640
HEAD_DIM = 64
GROUPS = 32
SINUS = 320
TIME_WIDTH = 1280
COLS = 256
ROW_CAP = 2
WINDOW = 8
TOTAL_ROWS = 20
N_PATCH = 16


def draw_latent(key, part):
    key = jax.random.fold_in(key, 11)
    key_base = jax.random.fold_in(key, 0)
    key_rows = jax.random.fold_in(key, 1)
    key_chans = jax.random.fold_in(key, 2)
    key_shift = jax.random.fold_in(key, 4)
    slots = N_PATCH * ROW_CAP
    base = jax.random.normal(key_base, (slots, COLS, CHANNELS), jnp.float32)
    offset = jax.random.uniform(key_shift, (1, 1, CHANNELS), jnp.float32, 0.6, 1.2)
    row_scale = jnp.exp(jax.random.uniform(key_rows, (slots, 1, 1), jnp.float32, -0.8, 0.8))
    chan_scale = jnp.exp(jax.random.uniform(key_chans, (1, 1, CHANNELS), jnp.float32, -0.7, 0.7))
    place = (jnp.arange(slots) // ROW_CAP).astype(jnp.float32) / (N_PATCH - 1)
    growth = 3.0
    rise = jnp.exp(math.log(growth) * place - 0.5)[:, None, None]
    return jnp.clip((base + offset) * row_scale * chan_scale * rise, -12.0, 12.0).astype(jnp.bfloat16)


def draw_stale_kv(key, part):
    key = jax.random.fold_in(key, 23)
    key_base = jax.random.fold_in(key, 0)
    total_tok = N_PATCH * ROW_CAP * COLS
    values = jax.random.normal(key_base, (total_tok, 2 * CHANNELS), jnp.float32)
    keys = values[:, :CHANNELS] * 2.0
    vals = values[:, CHANNELS:] * 4.0
    return jnp.clip(jnp.concatenate([keys, vals], axis=1), -100.0, 100.0).astype(jnp.bfloat16)


def draw_window(key, part):
    key = jax.random.fold_in(key, 37)
    bits = jax.random.randint(key, (N_PATCH, N_PATCH), 0, 2)
    lines = jnp.arange(N_PATCH)[:, None]
    others = jnp.arange(N_PATCH)[None, :]
    distance = jnp.abs(lines - others)
    pattern = jnp.where(distance == 0, 1, jnp.where(distance <= WINDOW, bits, 0))
    pattern = pattern.at[0, WINDOW].set(1)
    return pattern.astype(jnp.int32)


def length_profile(count, total, reach, lean):
    portions = [(1 << 20) // math.isqrt(standing ** lean) + 1 for standing in range(2, count + 1)]
    spare, given = total - reach - (count - 1), [1] * (count - 1)
    while spare > 0:
        candidates = [i for i in range(count - 1) if given[i] < reach]
        pool, remaining = sum([portions[i] for i in candidates]), spare
        for i in candidates:
            more = min(reach - given[i], max(1, remaining * portions[i] // pool), spare)
            given[i] = given[i] + more
            spare = spare - more
    return np.array([reach] + given)


def uneven_parts(key, count, total, reach, skew):
    if count == 2:
        one = jax.random.randint(key, (), max(1, total - reach), min(reach, total - 1) + 1)
        return jnp.stack([one, total - one])
    sizes = jnp.asarray(length_profile(count, total, reach, skew), jnp.int32)
    couples = (count - 1) // 2
    giver, sink = sizes[1:1 + 2 * couples:2], sizes[2:2 + 2 * couples:2]
    margin = jnp.minimum(giver - 1, reach - sink)
    shifted = jax.random.randint(jax.random.fold_in(key, 1), (couples,), 0, 1 << 20) % (margin + 1)
    sizes = sizes.at[1:1 + 2 * couples:2].set(giver - shifted).at[2:2 + 2 * couples:2].set(sink + shifted)
    return sizes[jax.random.permutation(jax.random.fold_in(key, 2), count)]


def gaussian(rng, shape, scale, limit, kind=jnp.bfloat16):
    drawn = scale * jax.random.normal(rng, shape, jnp.float32)
    return jnp.clip(drawn, min=-limit, max=limit).astype(kind)


def setup_inputs(seed: int = 0, part: int = 0) -> dict:
    seeds = jax.random.split(jax.random.key(seed), 13)
    part_keys = jax.random.split(jax.random.fold_in(seeds[12], part), 13)
    return {
        "latent": draw_latent(jax.random.fold_in(jax.random.fold_in(seeds[12], part), 71), part),
        "stale_kv": draw_stale_kv(jax.random.fold_in(jax.random.fold_in(seeds[12], part), 71), part),
        "row_counts": uneven_parts(part_keys[2], N_PATCH, TOTAL_ROWS, ROW_CAP, 2).astype(jnp.int32),
        "window": draw_window(jax.random.fold_in(jax.random.fold_in(seeds[12], part), 71), part),
        "time_index": jax.random.randint(part_keys[4], (1,), 0, 1000).astype(jnp.int32),
        "norm_gain": jnp.clip(1.0 + 0.15 * jax.random.normal(seeds[5], (CHANNELS,), jnp.float32), 0.25, 1.75).astype(jnp.bfloat16),
        "conv_weight": gaussian(seeds[6], (3, 3, CHANNELS, CHANNELS), (9 * CHANNELS) ** -0.5, 0.078125),
        "time_first": gaussian(seeds[7], (SINUS, TIME_WIDTH), SINUS ** -0.5, 0.3125),
        "time_second": gaussian(seeds[8], (TIME_WIDTH, CHANNELS), TIME_WIDTH ** -0.5, 0.15625),
        "attn_gain": jnp.clip(1.0 + 0.15 * jax.random.normal(seeds[9], (CHANNELS,), jnp.float32), 0.25, 1.75).astype(jnp.bfloat16),
        "attn_in": gaussian(seeds[10], (CHANNELS, 3 * CHANNELS), CHANNELS ** -0.5, 0.25),
        "attn_out": gaussian(seeds[11], (CHANNELS, CHANNELS), CHANNELS ** -0.5, 0.25),
    }


EPS = 1e-05
NEG = -1e+30

def time_vector(time_index, time_first, time_second):
    half = time_first.shape[0] // 2
    freqs = jnp.exp(-math.log(10000.0) * jnp.arange(half, dtype=jnp.float32) / half)
    angles = time_index.astype(jnp.float32)[0] * freqs
    sinus = jnp.concatenate([jnp.cos(angles), jnp.sin(angles)]).astype(jnp.bfloat16)
    hidden = jax.nn.silu(jnp.dot(sinus[None], time_first, preferred_element_type=jnp.float32)).astype(jnp.bfloat16)
    return jnp.dot(hidden, time_second, preferred_element_type=jnp.float32)[0]

def group_norm(values, valid, gain, count):
    chans = values.shape[-1]
    per = chans // GROUPS
    masked = values * valid
    sums = lax.optimization_barrier(jnp.sum(masked, axis=(0, 1))).reshape(GROUPS, per).sum(-1)
    mean_c = jnp.repeat(sums / count, per)
    centered = (values - mean_c) * valid
    spread = lax.optimization_barrier(jnp.sum(centered * centered, axis=(0, 1))).reshape(GROUPS, per).sum(-1) / count
    var_c = jnp.repeat(spread, per)
    normed = (values - mean_c) * lax.rsqrt(var_c + EPS) * gain.astype(jnp.float32)
    return (jax.nn.silu(normed) * valid).astype(jnp.bfloat16)

def attend(carry, query, block, allowed):
    best, total, acc = carry
    heads, tok, width = acc.shape
    keys = block[:, :heads * width].reshape(-1, heads, width).astype(jnp.float32)
    vals = block[:, heads * width:].reshape(-1, heads, width).astype(jnp.float32)
    scores = jnp.einsum('qhd,khd->hqk', query.astype(jnp.float32), keys, precision=lax.Precision.HIGHEST) * width ** (-0.5)
    scores = jnp.where(allowed[None, None, :], scores, NEG)
    new_best = jnp.maximum(best, scores.max(-1))
    shrink = jnp.exp(best - new_best)
    weights = jnp.exp(scores - new_best[..., None])
    total = total * shrink + weights.sum(-1)
    rounded = weights.astype(jnp.bfloat16).astype(jnp.float32)
    acc = acc * shrink[..., None] + jnp.einsum('hqk,khd->hqd', rounded, vals, precision=lax.Precision.HIGHEST)
    return (new_best, total, acc)

def reference(latent, stale_kv, row_counts, window, time_index, norm_gain, conv_weight, time_first, time_second, attn_gain, attn_in, attn_out):
    bands = row_counts.shape[0]
    slots, cols, chans = latent.shape
    rows = slots // bands
    band_tok = rows * cols
    heads = chans // HEAD_DIM
    counts = row_counts.astype(jnp.int32)
    live = jnp.arange(rows, dtype=jnp.int32)[None, :] < counts[:, None]
    valid = live.reshape(slots, 1, 1).astype(jnp.float32)
    total_rows = jnp.sum(counts)
    count = total_rows.astype(jnp.float32) * cols * (chans // GROUPS)
    tvec = time_vector(time_index, time_first, time_second)
    source = latent.astype(jnp.float32)
    first = group_norm(source, valid, norm_gain, count)
    starts = (jnp.cumsum(counts) - counts).astype(jnp.int32)
    image_rows = jnp.arange(TOTAL_ROWS, dtype=jnp.int32)
    band_of = (lax.optimization_barrier(jnp.sum((image_rows[:, None] >= starts[None, :]).astype(jnp.int32), axis=1)) - 1).astype(jnp.int32)
    source_rows = (band_of * rows + image_rows - starts[band_of]).astype(jnp.int32)
    image = first[source_rows].astype(jnp.float32)
    conv_image = lax.conv_general_dilated(image[None], conv_weight.astype(jnp.float32), (1, 1), ((1, 1), (1, 1)), dimension_numbers=('NHWC', 'HWIO', 'NHWC'), precision=lax.Precision.HIGHEST)[0]
    back = jnp.clip(starts[:, None] + jnp.arange(rows, dtype=jnp.int32)[None, :], 0, TOTAL_ROWS - 1).reshape(-1).astype(jnp.int32)
    conv = conv_image[back]
    resid = (source + conv + tvec).astype(jnp.bfloat16)
    second = group_norm(resid.astype(jnp.float32), valid, attn_gain, count)
    proj = jnp.dot(second.reshape(slots * cols, chans), attn_in, preferred_element_type=jnp.float32).astype(jnp.bfloat16)
    key_rows = jnp.arange(band_tok, dtype=jnp.int32) // cols

    def one_band(p):
        mine = lax.dynamic_slice_in_dim(proj, (p * band_tok).astype(jnp.int32), band_tok, 0)
        query = mine[:, :chans].reshape(band_tok, heads, HEAD_DIM)
        fresh = mine[:, chans:]

        def step(carry, j):
            stale = lax.dynamic_slice_in_dim(stale_kv, (j * band_tok).astype(jnp.int32), band_tok, 0)
            block = jnp.where(j == p, fresh, stale)
            allowed = key_rows < counts[j]
            active = window[p, j] == 1
            carry = lax.cond(active, lambda c: attend(c, query, block, allowed), lambda c: c, carry)
            return (carry, None)
        init = (jnp.full((heads, band_tok), NEG, jnp.float32), jnp.zeros((heads, band_tok), jnp.float32), jnp.zeros((heads, band_tok, HEAD_DIM), jnp.float32))
        (best, total, acc), _ = lax.scan(step, init, jnp.arange(bands, dtype=jnp.int32))
        out = acc / total[..., None]
        return out.transpose(1, 0, 2).reshape(band_tok, chans).astype(jnp.bfloat16)
    attended = lax.map(one_band, jnp.arange(bands, dtype=jnp.int32)).reshape(slots * cols, chans)
    update = jnp.dot(attended, attn_out, preferred_element_type=jnp.float32).reshape(slots, cols, chans)
    return ((resid.astype(jnp.float32) + update) * valid).astype(jnp.bfloat16)
```

```python
import math

import jax
import jax.numpy as jnp
import numpy as np
from jax import lax
from jax.experimental import pallas as pl
from jax.experimental.pallas import tpu as pltpu
from jax.sharding import PartitionSpec as P

HEAD_DIM = 64
GROUPS = 32
HEADS = 10
BANDS = 16
COLS = 256
CHANS = 640
TOK = 512
EPS = 1e-05
NEG = -1e30
MESH = pl.DeviceIdType.MESH
F32, BF16 = jnp.float32, jnp.bfloat16

OWNERS = ((0, 5, 10, 15, 1, 4, 11, 14, 3, 12), (0, 5, 10, 15, 2, 7, 8, 13, 6, 9))


def owner(head):
    core = lax.rem(lax.axis_index("batch"), 2)
    return OWNERS[0][head] + core * (OWNERS[1][head] - OWNERS[0][head])


def meet(me):
    barrier = pltpu.get_barrier_semaphore()

    @pl.loop(1, BANDS)
    def _(i):
        pl.semaphore_signal(
            barrier, inc=1, device_id={"patch": lax.rem(me + i, BANDS)}, device_id_type=MESH
        )

    return barrier


def remote(src, dst, send, recv, to):
    return pltpu.make_async_remote_copy(
        src, dst, send, recv, device_id={"patch": to}, device_id_type=MESH
    )


def lanes(shape):
    return lax.broadcasted_iota(jnp.int32, shape, 1)


def swap(x):
    return pltpu.roll(x, HEAD_DIM, 1)


def group_sum(vec, gmat):
    hi = vec.astype(BF16)
    rest = vec - hi.astype(F32)
    mid = rest.astype(BF16)
    low = (rest - mid.astype(F32)).astype(BF16)
    row = lax.broadcasted_iota(jnp.int32, (16, CHANS), 0)
    stack = jnp.where(
        row == 0,
        hi.astype(F32),
        jnp.where(row == 1, mid.astype(F32), jnp.where(row == 2, low.astype(F32), 0.0)),
    ).astype(BF16)
    out = jnp.dot(stack, gmat, preferred_element_type=F32)
    return jnp.sum(out, axis=0, keepdims=True)


def local_stats(x0, x1, live1, out_ref):
    tok = COLS * (1.0 + live1)
    sums = jnp.sum(x0, axis=0, keepdims=True) + live1 * jnp.sum(x1, axis=0, keepdims=True)
    mean = sums / tok
    d0, d1 = x0 - mean, x1 - mean
    spread = jnp.sum(d0 * d0, axis=0, keepdims=True) + live1 * jnp.sum(d1 * d1, axis=0, keepdims=True)
    out_ref[0:1, :] = sums
    out_ref[1:2, :] = spread


def merge_stats(stats_ref, counts_ref, gain, gmat):
    total = jnp.zeros((1, CHANS), F32)
    rows = 0
    for b in range(BANDS):
        total = total + stats_ref[b, 0:1, :]
        rows = rows + counts_ref[b]
    count = rows.astype(F32) * (COLS * (CHANS // GROUPS))
    mean = group_sum(total, gmat) / count
    spread = jnp.zeros((1, CHANS), F32)
    for b in range(BANDS):
        tok = counts_ref[b].astype(F32) * COLS
        off = stats_ref[b, 0:1, :] / tok - mean
        spread = spread + stats_ref[b, 1:2, :] + tok * (off * off)
    var = group_sum(spread, gmat) / count
    return mean, 0.5 * lax.rsqrt(var + EPS) * gain


def norm(x, mean, half):
    y = (x - mean) * half
    return y + y * jnp.tanh(y)


def ones_and_values(kv):
    return jnp.where(lanes(kv.shape) < HEAD_DIM, jnp.ones_like(kv), kv)


def to_lanes(column):
    eye = lax.broadcasted_iota(jnp.int32, (128, 128), 0) == lanes((128, 128))
    return jnp.sum(jnp.where(eye, column, 0.0), axis=0, keepdims=True)


def lead(
    counts_ref, time_ref, latent_ref, gain1_ref, gain2_ref, stale_hbm, conv_hbm, first_hbm, second_hbm, in_hbm, gmat_hbm,
    kv_all, q_all, resid_ref, own_ref, lse_ref,
    stale, wcat, wfirst, wsecond, win, gmat, halo_out, halo_in, stats_out, stats_in, x_ref, y_ref,
    kvp, qp, qs, kvf,
    local_sem, stat_send, stat_recv, halo_send, halo_recv, kv_send, kv_recv, q_send, q_recv,
):
    me = lax.axis_index("patch")
    up, down = lax.rem(me + 1, BANDS), lax.rem(me + BANDS - 1, BANDS)

    copies = {
        "stale": [(stale_hbm, stale)],
        "gmat": [(gmat_hbm, gmat)],
        "time": [(first_hbm, wfirst), (second_hbm, wsecond)],
        "conv": [
            (conv_hbm.at[dy, dx], wcat.at[pl.ds(dy * CHANS, CHANS), pl.ds(dx * CHANS, CHANS)])
            for dy in range(3)
            for dx in range(3)
        ],
        "in": [(in_hbm, win)],
    }
    copies = {
        name: [pltpu.make_async_copy(s, d, local_sem.at[i]) for s, d in pairs]
        for i, (name, pairs) in enumerate(copies.items())
    }
    for group in copies.values():
        for c in group:
            c.start()

    def arrived(name):
        for c in copies[name]:
            c.wait()

    barrier = meet(me)

    mine = counts_ref[me]
    live1 = (mine - 1).astype(F32)
    two = jnp.full((COLS, CHANS), mine, jnp.int32) == 2

    halo_out[...] = jnp.where(two, latent_ref[1], latent_ref[0])
    local_stats(latent_ref[0].astype(F32), latent_ref[1].astype(F32), live1, stats_out.at[0])
    stats_in[0, me] = stats_out[0]

    pl.semaphore_wait(barrier, BANDS - 1)

    def send_stats(turn):
        @pl.loop(1, BANDS)
        def _(i):
            to = lax.rem(me + i, BANDS)
            remote(
                stats_out.at[turn], stats_in.at[turn, me], stat_send.at[turn, to], stat_recv.at[turn, me], to
            ).start()

    def wait_stats(turn):
        @pl.loop(1, BANDS)
        def _(i):
            to = lax.rem(me + i, BANDS)
            c = remote(
                stats_out.at[turn], stats_in.at[turn, to], stat_send.at[turn, to], stat_recv.at[turn, to], to
            )
            c.wait_send()
            c.wait_recv()

    halos = (
        remote(halo_out, halo_in.at[0], halo_send.at[0], halo_recv.at[0], up),
        remote(latent_ref.at[0], halo_in.at[1], halo_send.at[1], halo_recv.at[1], down),
    )
    send_stats(0)
    for c in halos:
        c.start()

    arrived("stale")

    @pl.loop(0, HEADS // 2)
    def _(i):
        at = pl.multiple_of(i * 128, 128)
        keys = stale[:, pl.ds(at, 128)].astype(F32)
        vals = stale[:, pl.ds(pl.multiple_of(CHANS + i * 128, 128), 128)].astype(F32)
        low = lanes(keys.shape) < HEAD_DIM
        kvp[2 * i] = jnp.where(low, keys, swap(vals)).astype(BF16)
        kvp[2 * i + 1] = jnp.where(low, swap(keys), vals).astype(BF16)

    def to_owners(src, dst, send, recv, local):
        def far(h):
            return remote(src.at[h], dst.at[me], send.at[h], recv.at[me], owner(h))

        def near(h):
            return pltpu.make_async_copy(src.at[h], dst.at[me], local)

        def start():
            for h in range(HEADS):
                @pl.when(owner(h) != me)
                def _():
                    far(h).start()

                @pl.when(owner(h) == me)
                def _():
                    near(h).start()

        def wait():
            for h in range(HEADS):
                @pl.when(owner(h) != me)
                def _():
                    far(h).wait_send()

                @pl.when(owner(h) == me)
                def _():
                    near(h).wait()

                    @pl.loop(1, BANDS)
                    def _(i):
                        frm = lax.rem(me + i, BANDS)
                        remote(src.at[h], dst.at[frm], send.at[h], recv.at[frm], frm).wait_recv()

        return start, wait

    start_kv, wait_kv = to_owners(kvp, kv_all, kv_send, kv_recv, local_sem.at[5])
    start_q, wait_q = to_owners(qp, q_all, q_send, q_recv, local_sem.at[6])
    start_kv()

    arrived("time")
    half = wfirst.shape[0] // 2
    lane = lanes((8, 2 * half))
    k = jnp.where(lane < half, lane, lane - half).astype(F32)
    angles = time_ref[0].astype(F32) * jnp.exp(-math.log(10000.0) * k / half)
    sinus = jnp.where(lane < half, jnp.cos(angles), jnp.sin(angles)).astype(BF16)
    hidden = jnp.dot(sinus, wfirst[...], preferred_element_type=F32)
    hidden = (hidden / (1.0 + jnp.exp(-hidden))).astype(BF16)
    tvec = jnp.dot(hidden, wsecond[...], preferred_element_type=F32)[0:1, :]

    arrived("gmat")
    wait_stats(0)
    mean, scale = merge_stats(stats_in.at[0], counts_ref, gain1_ref[...], gmat[...])
    x_ref[0:COLS] = norm(latent_ref[0].astype(F32), mean, scale).astype(BF16)
    x_ref[COLS:TOK] = jnp.where(two, norm(latent_ref[1].astype(F32), mean, scale), 0.0).astype(BF16)

    arrived("conv")
    chunk = 256
    whole = 3 * CHANS // chunk

    def each_chunk(step):
        @pl.loop(0, whole)
        def _(i):
            step(pl.ds(pl.multiple_of(i * chunk, chunk), chunk))

        step(slice(whole * chunk, 3 * CHANS))

    def own_rows(at):
        mid = jnp.dot(x_ref[...], wcat[CHANS : 2 * CHANS, at], preferred_element_type=F32)
        under = jnp.dot(x_ref[COLS:TOK], wcat[2 * CHANS :, at], preferred_element_type=F32)
        over = jnp.dot(x_ref[0:COLS], wcat[0:CHANS, at], preferred_element_type=F32)
        y_ref[0:COLS, at] = mid[0:COLS] + under
        y_ref[COLS:TOK, at] = mid[COLS:TOK] + over

    each_chunk(own_rows)
    for c in halos:
        c.wait()
    x_ref[0:COLS] = jnp.where(
        jnp.full((COLS, CHANS), me, jnp.int32) > 0, norm(halo_in[0].astype(F32), mean, scale), 0.0
    ).astype(BF16)
    x_ref[COLS:TOK] = jnp.where(
        jnp.full((COLS, CHANS), me, jnp.int32) < BANDS - 1, norm(halo_in[1].astype(F32), mean, scale), 0.0
    ).astype(BF16)

    def other_rows(at):
        over = jnp.dot(x_ref[0:COLS], wcat[0:CHANS, at], preferred_element_type=F32)
        under = jnp.dot(x_ref[COLS:TOK], wcat[2 * CHANS :, at], preferred_element_type=F32)
        both = jnp.full(under.shape, mine, jnp.int32) == 2
        y_ref[0:COLS, at] = y_ref[0:COLS, at] + over + jnp.where(both, 0.0, under)
        y_ref[COLS:TOK, at] = y_ref[COLS:TOK, at] + jnp.where(both, under, 0.0)

    each_chunk(other_rows)
    row = lax.broadcasted_iota(jnp.int32, (COLS, CHANS), 0)
    for r in range(2):
        here = slice(r * COLS, (r + 1) * COLS)
        left = pltpu.roll(y_ref[here, 0:CHANS], 1, 0)
        right = pltpu.roll(y_ref[here, 2 * CHANS :], COLS - 1, 0)
        conv = y_ref[here, CHANS : 2 * CHANS] + jnp.where(row == 0, 0.0, left) + jnp.where(
            row == COLS - 1, 0.0, right
        )
        resid_ref[here, :] = (latent_ref[r].astype(F32) + conv + tvec).astype(BF16)

    local_stats(resid_ref[0:COLS].astype(F32), resid_ref[COLS:TOK].astype(F32), live1, stats_out.at[1])
    stats_in[1, me] = stats_out[1]
    send_stats(1)
    arrived("in")
    wait_stats(1)
    mean, scale = merge_stats(stats_in.at[1], counts_ref, gain2_ref[...], gmat[...])
    x_ref[0:COLS] = norm(resid_ref[0:COLS].astype(F32), mean, scale).astype(BF16)
    x_ref[COLS:TOK] = jnp.where(two, norm(resid_ref[COLS:TOK].astype(F32), mean, scale), 0.0).astype(BF16)

    fold = HEAD_DIM**-0.5 * math.log2(math.e)
    query = jnp.dot(x_ref[...], win[:, 0:CHANS], preferred_element_type=F32) * fold
    low = lanes((TOK, 128)) < HEAD_DIM
    for i in range(HEADS // 2):
        pair = query[:, i * 128 : (i + 1) * 128]
        turned = swap(pair)
        qs[2 * i] = jnp.where(low, pair, 0.0).astype(BF16)
        qs[2 * i + 1] = jnp.where(low, turned, 0.0).astype(BF16)
        qp[2 * i] = jnp.where(low[0:COLS], pair[0:COLS], turned[COLS:TOK]).astype(BF16)
        qp[2 * i + 1] = jnp.where(low[0:COLS], turned[0:COLS], pair[COLS:TOK]).astype(BF16)
    start_q()

    keys = jnp.dot(x_ref[...], win[:, CHANS : 2 * CHANS], preferred_element_type=F32)
    vals = jnp.dot(x_ref[...], win[:, 2 * CHANS :], preferred_element_type=F32)
    for i in range(HEADS // 2):
        kt, vt = keys[:, i * 128 : (i + 1) * 128], vals[:, i * 128 : (i + 1) * 128]
        kvf[2 * i] = jnp.where(low, kt, swap(vt)).astype(BF16)
        kvf[2 * i + 1] = jnp.where(low, swap(kt), vt).astype(BF16)

    @pl.loop(0, HEADS // 2)
    def _(i):
        for r in range(2):
            here = pl.ds(r * COLS, COLS)
            outs = []
            for sub in range(2):
                h = 2 * i + sub
                kv = kvf[h]
                s = lax.dot_general(
                    qs[h, here], kv, (((1,), (1,)), ((), ())), preferred_element_type=F32
                )
                dead = (lanes(s.shape) >= COLS) & (jnp.full(s.shape, mine, jnp.int32) < 2)
                s = jnp.where(dead, NEG, s)
                best = jnp.max(s, axis=1, keepdims=True)
                acc = jnp.dot(
                    jnp.exp2(s - best).astype(BF16), ones_and_values(kv), preferred_element_type=F32
                )
                turned = swap(acc)
                first = lanes(acc.shape) < HEAD_DIM
                total = jnp.where(first, acc, turned)
                lse = best + jnp.log2(total)
                lse_ref[h, 2 * r : 2 * r + 1, :] = to_lanes(lse[0:128])
                lse_ref[h, 2 * r + 1 : 2 * r + 2, :] = to_lanes(lse[128:256])
                outs.append((turned if sub == 0 else acc) / total)
            own_ref[here, pl.ds(pl.multiple_of(i * 128, 128), 128)] = jnp.where(
                lanes((COLS, 128)) < HEAD_DIM, outs[0], outs[1]
            ).astype(BF16)

    wait_kv()
    wait_q()


def attend(counts_ref, window_ref, q_ref, kv_ref, o_ref, lse_ref, list_ref, qs, s_ref, best_ref, acc_ref):
    me = lax.axis_index("patch")
    mine = owner(0) == me
    for h in range(1, HEADS):
        mine = jnp.logical_or(mine, owner(h) == me)

    def band(p):
        n = jnp.int32(0)
        for j in range(BANDS):
            seen = jnp.where(jnp.logical_and(window_ref[p, j] == 1, p != j), 1, 0)
            list_ref[n] = 2 * j
            n = n + seen
            list_ref[n] = 2 * j + 1
            n = n + seen * (counts_ref[j] - 1)

        def process(rows):
            tok = rows * COLS
            q = q_ref[p].astype(F32)
            low = lanes((COLS, 128)) < HEAD_DIM
            qs[0:COLS] = jnp.where(low, q, 0.0).astype(BF16)
            if rows == 2:
                qs[COLS:TOK] = jnp.where(low, swap(q), 0.0).astype(BF16)
            best_ref[0:tok] = jnp.full((tok, 128), NEG, F32)
            acc_ref[0:tok] = jnp.zeros((tok, 128), F32)

            @pl.loop(0, n)
            def _(k):
                s = lax.dot_general(
                    qs[0:tok], kv_ref[list_ref[k]], (((1,), (1,)), ((), ())), preferred_element_type=F32
                )
                s_ref[k, 0:tok] = s
                best_ref[0:tok] = jnp.maximum(best_ref[0:tok], jnp.maximum(s[:, 0:128], s[:, 128:256]))

            best = jnp.max(best_ref[0:tok], axis=1, keepdims=True)
            best_ref[0:tok] = jnp.broadcast_to(best, (tok, 128))

            @pl.loop(0, n)
            def _(k):
                top = best_ref[0:tok]
                s = s_ref[k, 0:tok]
                w = jnp.concatenate([jnp.exp2(s[:, 0:128] - top), jnp.exp2(s[:, 128:256] - top)], axis=1)
                acc_ref[0:tok] += jnp.dot(
                    w.astype(BF16), ones_and_values(kv_ref[list_ref[k]]), preferred_element_type=F32
                )

            outs = []
            for r in range(rows):
                here = slice(r * COLS, (r + 1) * COLS)
                acc = acc_ref[here]
                turned = swap(acc)
                total = jnp.where(low, acc, turned)
                some = total > 0.0
                safe = jnp.where(some, total, 1.0)
                lse = jnp.where(some, best_ref[here] + jnp.log2(safe), NEG)
                lse_ref[p, 2 * r : 2 * r + 1, :] = to_lanes(lse[0:128])
                lse_ref[p, 2 * r + 1 : 2 * r + 2, :] = to_lanes(lse[128:256])
                outs.append((turned if r == 0 else acc) / safe)
            if rows == 1:
                outs.append(outs[0])
                lse_ref[p, 2:4, :] = lse_ref[p, 0:2, :]
            o_ref[p] = jnp.where(low, outs[0], outs[1]).astype(BF16)

        @pl.when(counts_ref[p] == 1)
        def _():
            process(1)

        @pl.when(counts_ref[p] == 2)
        def _():
            process(2)

    @pl.when(mine)
    def _():
        @pl.loop(0, BANDS)
        def _(p):
            band(p)


def tail(
    counts_ref, o_ref, lse_ref, resid_ref, own_ref, own_lse_ref, out_hbm, mixed_ref,
    wout, o_in, lse_in, sig_ref, att_ref,
    local_sem, o_send, o_recv, l_send, l_recv,
):
    me = lax.axis_index("patch")
    barrier = meet(me)
    weights = pltpu.make_async_copy(out_hbm, wout, local_sem.at[0])
    weights.start()
    pl.semaphore_wait(barrier, BANDS - 1)

    for h in range(HEADS):
        @pl.when(owner(h) == me)
        def _():
            @pl.loop(1, BANDS)
            def _(i):
                to = lax.rem(me + i, BANDS)
                remote(o_ref.at[to], o_in.at[h], o_send.at[to], o_recv.at[h], to).start()
                remote(lse_ref.at[to], lse_in.at[h], l_send.at[to], l_recv.at[h], to).start()

            o_in[h] = o_ref[me]
            lse_in[h] = lse_ref[me]

    weights.wait()
    for h in range(HEADS):
        @pl.when(owner(h) != me)
        def _():
            frm = owner(h)
            remote(o_ref.at[0], o_in.at[h], o_send.at[0], o_recv.at[h], frm).wait_recv()
            remote(lse_ref.at[0], lse_in.at[h], l_send.at[0], l_recv.at[h], frm).wait_recv()

    sig_ref[...] = jnp.zeros_like(sig_ref)
    for h in range(HEADS):
        sig_ref[4 * h : 4 * h + 4, :] = 1.0 / (1.0 + jnp.exp2(own_lse_ref[h] - lse_in[h]))

    low = lanes((COLS, 128)) < HEAD_DIM
    for i in range(HEADS // 2):
        a, b = o_in[2 * i].astype(F32), o_in[2 * i + 1].astype(F32)
        at = slice(i * 128, (i + 1) * 128)
        att_ref[0:COLS, at] = jnp.where(low, a, swap(b))
        att_ref[COLS:TOK, at] = jnp.where(low, swap(a), b)

    spread = (lanes((16, CHANS)) // HEAD_DIM == lax.broadcasted_iota(jnp.int32, (16, CHANS), 0)).astype(F32).astype(BF16)
    mine = counts_ref[me]
    for blk in range(4):
        here = slice(blk * 128, (blk + 1) * 128)
        sig = sig_ref[pl.ds(blk, 16, stride=4), :]
        hi = sig.astype(BF16)
        lo = (sig - hi.astype(F32)).astype(BF16)
        dims = (((0,), (0,)), ((), ()))
        share = lax.dot_general(hi, spread, dims, preferred_element_type=F32) + lax.dot_general(
            lo, spread, dims, preferred_element_type=F32
        )
        own = own_ref[here].astype(F32)
        att = (own + (att_ref[here] - own) * share).astype(BF16)
        update = jnp.dot(att, wout[...], preferred_element_type=F32)
        mixed = resid_ref[here].astype(F32) + update
        if blk >= 2:
            mixed = jnp.where(jnp.full(mixed.shape, mine, jnp.int32) == 2, mixed, 0.0)
        mixed_ref[blk // 2, (blk % 2) * 128 : (blk % 2) * 128 + 128, :] = mixed.astype(BF16)

    for h in range(HEADS):
        @pl.when(owner(h) == me)
        def _():
            @pl.loop(1, BANDS)
            def _(i):
                to = lax.rem(me + i, BANDS)
                remote(o_ref.at[to], o_in.at[h], o_send.at[to], o_recv.at[h], to).wait_send()
                remote(lse_ref.at[to], lse_in.at[h], l_send.at[to], l_recv.at[h], to).wait_send()


def body(
    latent, stale_kv, row_counts, window, time_index, norm_gain, conv_weight, time_first, time_second, attn_gain,
    attn_in, attn_out,
):
    smem = pl.BlockSpec(memory_space=pltpu.SMEM)
    vmem = pl.BlockSpec(memory_space=pltpu.VMEM)
    hbm = pl.BlockSpec(memory_space=pl.ANY)
    dma = pltpu.SemaphoreType.DMA
    shape = jax.ShapeDtypeStruct
    group = np.arange(CHANS) // (CHANS // GROUPS)
    gmat = jnp.asarray(group[:, None] == group[None, :], BF16)
    kv_all, q_all, resid, own, own_lse = pl.pallas_call(
        lead,
        out_shape=(
            shape((BANDS, TOK, 128), BF16),
            shape((BANDS, COLS, 128), BF16),
            shape((TOK, CHANS), BF16),
            shape((TOK, CHANS), BF16),
            shape((HEADS, 4, 128), F32),
        ),
        in_specs=[smem, smem, vmem, vmem, vmem] + [hbm] * 6,
        out_specs=(hbm, hbm, vmem, vmem, vmem),
        scratch_shapes=[
            pltpu.VMEM((TOK, 2 * CHANS), BF16),
            pltpu.VMEM((3 * CHANS, 3 * CHANS), BF16),
            pltpu.VMEM(time_first.shape, BF16),
            pltpu.VMEM(time_second.shape, BF16),
            pltpu.VMEM((CHANS, 3 * CHANS), BF16),
            pltpu.VMEM((CHANS, CHANS), BF16),
            pltpu.VMEM((COLS, CHANS), BF16),
            pltpu.VMEM((2, COLS, CHANS), BF16),
            pltpu.VMEM((2, 2, CHANS), F32),
            pltpu.VMEM((2, BANDS, 2, CHANS), F32),
            pltpu.VMEM((TOK, CHANS), BF16),
            pltpu.VMEM((TOK, 3 * CHANS), F32),
            pltpu.VMEM((HEADS, TOK, 128), BF16),
            pltpu.VMEM((HEADS, COLS, 128), BF16),
            pltpu.VMEM((HEADS, TOK, 128), BF16),
            pltpu.VMEM((HEADS, TOK, 128), BF16),
            dma((7,)),
            dma((2, BANDS)),
            dma((2, BANDS)),
            dma((2,)),
            dma((2,)),
            dma((HEADS,)),
            dma((BANDS,)),
            dma((HEADS,)),
            dma((BANDS,)),
        ],
        compiler_params=pltpu.CompilerParams(
            collective_id=0, has_side_effects=True, vmem_limit_bytes=56 << 20
        ),
        name="lead",
    )(
        row_counts, time_index, latent, norm_gain[None].astype(F32), attn_gain[None].astype(F32), stale_kv,
        conv_weight, time_first, time_second, attn_in, gmat,
    )
    o_all, lse_all = pl.pallas_call(
        attend,
        out_shape=(shape((BANDS, COLS, 128), BF16), shape((BANDS, 4, 128), F32)),
        in_specs=[smem, smem, vmem, vmem],
        out_specs=(vmem, vmem),
        scratch_shapes=[
            pltpu.SMEM((2 * BANDS + 8,), jnp.int32),
            pltpu.VMEM((TOK, 128), BF16),
            pltpu.VMEM((2 * BANDS, TOK, COLS), F32),
            pltpu.VMEM((TOK, 128), F32),
            pltpu.VMEM((TOK, 128), F32),
        ],
        compiler_params=pltpu.CompilerParams(vmem_limit_bytes=56 << 20),
        name="attend",
    )(row_counts, window, q_all, kv_all.reshape(2 * BANDS, COLS, 128))
    return pl.pallas_call(
        tail,
        out_shape=shape((2, COLS, CHANS), BF16),
        in_specs=[smem] + [vmem] * 5 + [hbm],
        out_specs=vmem,
        scratch_shapes=[
            pltpu.VMEM((CHANS, CHANS), BF16),
            pltpu.VMEM((HEADS, COLS, 128), BF16),
            pltpu.VMEM((HEADS, 4, 128), F32),
            pltpu.VMEM((64, 128), F32),
            pltpu.VMEM((TOK, CHANS), F32),
            dma((1,)),
            dma((BANDS,)),
            dma((HEADS,)),
            dma((BANDS,)),
            dma((HEADS,)),
        ],
        compiler_params=pltpu.CompilerParams(
            collective_id=1, has_side_effects=True, vmem_limit_bytes=56 << 20
        ),
        name="tail",
    )(row_counts, o_all, lse_all, resid, own, own_lse, attn_out)


def solution(mesh):
    part = P(("batch", "patch"))
    placed = (part, part, P("batch"), P("batch"), P("batch")) + (P(),) * 7
    return jax.shard_map(body, mesh=mesh, in_specs=placed, out_specs=part, check_vma=False)
```

```python
import math

import jax
import jax.numpy as jnp
import numpy as np
from jax import lax
from jax.experimental import pallas as pl
from jax.experimental.pallas import tpu as pltpu
from jax.sharding import PartitionSpec as P

HEAD_DIM = 64
GROUPS = 32
HEADS = 10
BANDS = 16
COLS = 256
CHANS = 640
TOK = 512
EPS = 1e-05
NEG = -1e30
MESH = pl.DeviceIdType.MESH
F32, BF16 = jnp.float32, jnp.bfloat16

OWNERS = ((0, 5, 10, 15, 1, 4, 11, 14, 3, 12), (0, 5, 10, 15, 2, 7, 8, 13, 6, 9))


def owner(head):
    core = lax.rem(lax.axis_index("batch"), 2)
    return OWNERS[0][head] + core * (OWNERS[1][head] - OWNERS[0][head])


def meet(me):
    barrier = pltpu.get_barrier_semaphore()

    @pl.loop(1, BANDS)
    def _(i):
        pl.semaphore_signal(
            barrier, inc=1, device_id={"patch": lax.rem(me + i, BANDS)}, device_id_type=MESH
        )

    return barrier


def remote(src, dst, send, recv, to):
    return pltpu.make_async_remote_copy(
        src, dst, send, recv, device_id={"patch": to}, device_id_type=MESH
    )


def lanes(shape):
    return lax.broadcasted_iota(jnp.int32, shape, 1)


def swap(x):
    return pltpu.roll(x, HEAD_DIM, 1)


def group_sum(vec, gmat):
    hi = vec.astype(BF16)
    rest = vec - hi.astype(F32)
    mid = rest.astype(BF16)
    low = (rest - mid.astype(F32)).astype(BF16)
    row = lax.broadcasted_iota(jnp.int32, (16, CHANS), 0)
    stack = jnp.where(
        row == 0,
        hi.astype(F32),
        jnp.where(row == 1, mid.astype(F32), jnp.where(row == 2, low.astype(F32), 0.0)),
    ).astype(BF16)
    out = jnp.dot(stack, gmat, preferred_element_type=F32)
    return jnp.sum(out, axis=0, keepdims=True)


def local_stats(x0, x1, live1, out_ref):
    tok = COLS * (1.0 + live1)
    sums = jnp.sum(x0, axis=0, keepdims=True) + live1 * jnp.sum(x1, axis=0, keepdims=True)
    mean = sums / tok
    d0, d1 = x0 - mean, x1 - mean
    spread = jnp.sum(d0 * d0, axis=0, keepdims=True) + live1 * jnp.sum(d1 * d1, axis=0, keepdims=True)
    out_ref[0:1, :] = sums
    out_ref[1:2, :] = spread


def merge_stats(stats_ref, counts_ref, gain, gmat):
    total = jnp.zeros((1, CHANS), F32)
    rows = 0
    for b in range(BANDS):
        total = total + stats_ref[b, 0:1, :]
        rows = rows + counts_ref[b]
    count = rows.astype(F32) * (COLS * (CHANS // GROUPS))
    mean = group_sum(total, gmat) / count
    spread = jnp.zeros((1, CHANS), F32)
    for b in range(BANDS):
        tok = counts_ref[b].astype(F32) * COLS
        off = stats_ref[b, 0:1, :] / tok - mean
        spread = spread + stats_ref[b, 1:2, :] + tok * (off * off)
    var = group_sum(spread, gmat) / count
    return mean, 0.5 * lax.rsqrt(var + EPS) * gain


def norm(x, mean, half):
    y = (x - mean) * half
    return y + y * jnp.tanh(y)


def side_by_side(x):
    turned = swap(x)
    low = lanes((COLS, 128)) < HEAD_DIM
    return jnp.where(low, x[0:COLS], turned[COLS:TOK]), jnp.where(low, turned[0:COLS], x[COLS:TOK])


def lead(
    counts_ref, time_ref, latent_ref, gain1_ref, gain2_ref, stale_hbm, conv_hbm, first_hbm, second_hbm, in_hbm, gmat_hbm,
    kv_all, q_all, resid_ref, own_ref, lse_ref,
    stale, wcat, wfirst, wsecond, win, gmat, halo_out, halo_in, stats_out, stats_in, x_ref, y_ref,
    kvp, qp, qs, kf, vt,
    local_sem, stat_send, stat_recv, halo_send, halo_recv, kv_send, kv_recv, q_send, q_recv,
):
    me = lax.axis_index("patch")
    up, down = lax.rem(me + 1, BANDS), lax.rem(me + BANDS - 1, BANDS)

    copies = {
        "stale": [(stale_hbm, stale)],
        "gmat": [(gmat_hbm, gmat)],
        "time": [(first_hbm, wfirst), (second_hbm, wsecond)],
        "conv": [
            (conv_hbm.at[dy, dx], wcat.at[pl.ds(dy * CHANS, CHANS), pl.ds(dx * CHANS, CHANS)])
            for dy in range(3)
            for dx in range(3)
        ],
        "in": [(in_hbm, win)],
    }
    copies = {
        name: [pltpu.make_async_copy(s, d, local_sem.at[i]) for s, d in pairs]
        for i, (name, pairs) in enumerate(copies.items())
    }
    for group in copies.values():
        for c in group:
            c.start()

    def arrived(name):
        for c in copies[name]:
            c.wait()

    barrier = meet(me)

    mine = counts_ref[me]
    live1 = (mine - 1).astype(F32)
    two = jnp.full((COLS, CHANS), mine, jnp.int32) == 2

    halo_out[...] = jnp.where(two, latent_ref[1], latent_ref[0])
    local_stats(latent_ref[0].astype(F32), latent_ref[1].astype(F32), live1, stats_out.at[0])
    stats_in[0, me] = stats_out[0]

    pl.semaphore_wait(barrier, BANDS - 1)

    def send_stats(turn):
        @pl.loop(1, BANDS)
        def _(i):
            to = lax.rem(me + i, BANDS)
            remote(
                stats_out.at[turn], stats_in.at[turn, me], stat_send.at[turn, to], stat_recv.at[turn, me], to
            ).start()

    def wait_stats(turn):
        @pl.loop(1, BANDS)
        def _(i):
            to = lax.rem(me + i, BANDS)
            c = remote(
                stats_out.at[turn], stats_in.at[turn, to], stat_send.at[turn, to], stat_recv.at[turn, to], to
            )
            c.wait_send()
            c.wait_recv()

    halos = (
        remote(halo_out, halo_in.at[0], halo_send.at[0], halo_recv.at[0], up),
        remote(latent_ref.at[0], halo_in.at[1], halo_send.at[1], halo_recv.at[1], down),
    )
    send_stats(0)
    for c in halos:
        c.start()

    arrived("stale")

    @pl.loop(0, HEADS // 2)
    def _(i):
        at = pl.multiple_of(i * 128, 128)
        keys = side_by_side(stale[:, pl.ds(at, 128)].astype(F32))
        vals = stale[:, pl.ds(pl.multiple_of(CHANS + i * 128, 128), 128)].astype(F32).T
        for sub in range(2):
            h = 2 * i + sub
            kvp[h, 0:COLS] = keys[sub].astype(BF16)
            for blk in range(4):
                kvp[h, COLS + blk * HEAD_DIM : COLS + (blk + 1) * HEAD_DIM] = vals[
                    sub * HEAD_DIM : (sub + 1) * HEAD_DIM, blk * 128 : (blk + 1) * 128
                ].astype(BF16)

    def to_owners(src, dst, send, recv, local):
        def far(h):
            return remote(src.at[h], dst.at[me], send.at[h], recv.at[me], owner(h))

        def near(h):
            return pltpu.make_async_copy(src.at[h], dst.at[me], local)

        def send_to(i):
            to = lax.rem(me + i, BANDS)
            head, found = jnp.int32(0), jnp.int32(0)
            for h in range(HEADS):
                hit = jnp.where(owner(h) == to, 1, 0)
                head, found = head + h * hit, found + hit

            @pl.when(found == 1)
            def _():
                remote(src.at[head], dst.at[me], send.at[head], recv.at[me], to).start()

        def start_column():
            for i in (4, 8, 12):
                send_to(i)
            for h in range(HEADS):
                @pl.when(owner(h) == me)
                def _():
                    near(h).start()

        def start_rest():
            @pl.loop(1, BANDS)
            def _(i):
                @pl.when(lax.rem(i, 4) != 0)
                def _():
                    send_to(i)

        def wait():
            for h in range(HEADS):
                @pl.when(owner(h) != me)
                def _():
                    far(h).wait_send()

                @pl.when(owner(h) == me)
                def _():
                    near(h).wait()

                    @pl.loop(1, BANDS)
                    def _(i):
                        frm = lax.rem(me + i, BANDS)
                        remote(src.at[h], dst.at[frm], send.at[h], recv.at[frm], frm).wait_recv()

        return start_column, start_rest, wait

    column_kv, rest_kv, wait_kv = to_owners(kvp, kv_all, kv_send, kv_recv, local_sem.at[5])
    column_q, rest_q, wait_q = to_owners(qp, q_all, q_send, q_recv, local_sem.at[6])

    column_kv()

    arrived("time")
    half = wfirst.shape[0] // 2
    lane = lanes((8, 2 * half))
    k = jnp.where(lane < half, lane, lane - half).astype(F32)
    angles = time_ref[0].astype(F32) * jnp.exp(-math.log(10000.0) * k / half)
    sinus = jnp.where(lane < half, jnp.cos(angles), jnp.sin(angles)).astype(BF16)
    hidden = jnp.dot(sinus, wfirst[...], preferred_element_type=F32)
    hidden = (hidden / (1.0 + jnp.exp(-hidden))).astype(BF16)
    tvec = jnp.dot(hidden, wsecond[...], preferred_element_type=F32)[0:1, :]

    arrived("gmat")
    wait_stats(0)
    mean, scale = merge_stats(stats_in.at[0], counts_ref, gain1_ref[...].astype(F32)[None], gmat[...])
    x_ref[0:COLS] = norm(latent_ref[0].astype(F32), mean, scale).astype(BF16)
    x_ref[COLS:TOK] = jnp.where(two, norm(latent_ref[1].astype(F32), mean, scale), 0.0).astype(BF16)

    arrived("conv")
    chunk = 256
    whole = 3 * CHANS // chunk

    def each_chunk(step):
        @pl.loop(0, whole)
        def _(i):
            step(pl.ds(pl.multiple_of(i * chunk, chunk), chunk))

        step(slice(whole * chunk, 3 * CHANS))

    def own_rows(at):
        mid = jnp.dot(x_ref[...], wcat[CHANS : 2 * CHANS, at], preferred_element_type=F32)
        under = jnp.dot(x_ref[COLS:TOK], wcat[2 * CHANS :, at], preferred_element_type=F32)
        over = jnp.dot(x_ref[0:COLS], wcat[0:CHANS, at], preferred_element_type=F32)
        y_ref[0:COLS, at] = mid[0:COLS] + under
        y_ref[COLS:TOK, at] = mid[COLS:TOK] + over

    each_chunk(own_rows)
    for c in halos:
        c.wait()
    rest_kv()
    x_ref[0:COLS] = jnp.where(
        jnp.full((COLS, CHANS), me, jnp.int32) > 0, norm(halo_in[0].astype(F32), mean, scale), 0.0
    ).astype(BF16)
    x_ref[COLS:TOK] = jnp.where(
        jnp.full((COLS, CHANS), me, jnp.int32) < BANDS - 1, norm(halo_in[1].astype(F32), mean, scale), 0.0
    ).astype(BF16)

    def other_rows(at):
        over = jnp.dot(x_ref[0:COLS], wcat[0:CHANS, at], preferred_element_type=F32)
        under = jnp.dot(x_ref[COLS:TOK], wcat[2 * CHANS :, at], preferred_element_type=F32)
        both = jnp.full(under.shape, mine, jnp.int32) == 2
        y_ref[0:COLS, at] = y_ref[0:COLS, at] + over + jnp.where(both, 0.0, under)
        y_ref[COLS:TOK, at] = y_ref[COLS:TOK, at] + jnp.where(both, under, 0.0)

    each_chunk(other_rows)
    row = lax.broadcasted_iota(jnp.int32, (COLS, CHANS), 0)
    for r in range(2):
        here = slice(r * COLS, (r + 1) * COLS)
        left = pltpu.roll(y_ref[here, 0:CHANS], 1, 0)
        right = pltpu.roll(y_ref[here, 2 * CHANS :], COLS - 1, 0)
        conv = y_ref[here, CHANS : 2 * CHANS] + jnp.where(row == 0, 0.0, left) + jnp.where(
            row == COLS - 1, 0.0, right
        )
        resid_ref[here, :] = (latent_ref[r].astype(F32) + conv + tvec).astype(BF16)

    local_stats(resid_ref[0:COLS].astype(F32), resid_ref[COLS:TOK].astype(F32), live1, stats_out.at[1])
    stats_in[1, me] = stats_out[1]
    send_stats(1)
    arrived("in")
    wait_stats(1)
    mean, scale = merge_stats(stats_in.at[1], counts_ref, gain2_ref[...].astype(F32)[None], gmat[...])
    x_ref[0:COLS] = norm(resid_ref[0:COLS].astype(F32), mean, scale).astype(BF16)
    x_ref[COLS:TOK] = jnp.where(two, norm(resid_ref[COLS:TOK].astype(F32), mean, scale), 0.0).astype(BF16)

    fold = HEAD_DIM**-0.5 * math.log2(math.e)
    query = jnp.dot(x_ref[...], win[:, 0:CHANS], preferred_element_type=F32) * fold
    low = lanes((TOK, 128)) < HEAD_DIM
    for i in range(HEADS // 2):
        pair = query[:, i * 128 : (i + 1) * 128]
        qs[2 * i] = jnp.where(low, pair, 0.0).astype(BF16)
        qs[2 * i + 1] = jnp.where(low, 0.0, pair).astype(BF16)
        for sub, packed in enumerate(side_by_side(pair)):
            qp[2 * i + sub] = packed.astype(BF16)
    rest_q()
    column_q()

    kf[...] = jnp.dot(x_ref[...], win[:, CHANS : 2 * CHANS], preferred_element_type=F32).astype(BF16)
    vals = jnp.dot(x_ref[...], win[:, 2 * CHANS :], preferred_element_type=F32)
    for i in range(HEADS // 2):
        vt[i * 128 : (i + 1) * 128] = vals[:, i * 128 : (i + 1) * 128].T.astype(BF16)
    shut = jnp.where(mine == 2, 0.0, NEG)
    ones = jnp.ones((16, TOK), BF16)

    @pl.loop(0, HEADS // 2)
    def _(i):
        keys = kf[:, pl.ds(pl.multiple_of(i * 128, 128), 128)]
        for sub in range(2):
            h = 2 * i + sub
            chans = pl.ds(pl.multiple_of(h * HEAD_DIM, HEAD_DIM), HEAD_DIM)
            values = jnp.concatenate([vt[chans], ones], axis=0)
            for r in range(2):
                here = slice(r * COLS, (r + 1) * COLS)
                s = lax.dot_general(
                    keys, qs[h, here], (((1,), (1,)), ((), ())), preferred_element_type=F32
                )
                s0, s1 = s[0:COLS], s[COLS:TOK] + shut
                best = jnp.max(jnp.maximum(s0, s1), axis=0, keepdims=True)
                w = jnp.concatenate([jnp.exp2(s0 - best), jnp.exp2(s1 - best)], axis=0).astype(BF16)
                acc = jnp.dot(values, w, preferred_element_type=F32)
                total = acc[HEAD_DIM : HEAD_DIM + 1]
                own_ref[chans, here] = (acc[0:HEAD_DIM] / total).astype(BF16)
                lse_ref[h, r : r + 1, :] = best + jnp.log2(total)

    wait_kv()
    wait_q()


STEP = 4
AHEAD = 4
LIST = 24


def attend(
    counts_ref, window_ref, q_hbm, kv_hbm, o_ref, lse_ref,
    q_ref, kv_ref, local_sem, keys_list, step_q, step_k, step_left, step_flag, kx, qx, vx, s_ref, top_ref, best_ref, acc_ref,
):
    me = lax.axis_index("patch")
    mine = owner(0) == me
    for h in range(1, HEADS):
        mine = jnp.logical_or(mine, owner(h) == me)
    low = lanes((COLS, 128)) < HEAD_DIM

    def unpack(j):
        ones = jnp.ones((16, COLS), BF16)

        def values(r):
            at = COLS + 2 * r * HEAD_DIM
            pair = [kv_ref[j, at : at + HEAD_DIM], kv_ref[j, at + HEAD_DIM : at + 2 * HEAD_DIM]]
            return jnp.concatenate([jnp.concatenate(pair, axis=1), ones], axis=0)

        keys, q = kv_ref[j, 0:COLS], q_ref[j]
        kx[2 * j] = keys
        qx[2 * j] = jnp.where(low, q, jnp.zeros_like(q))
        vx[2 * j] = values(0)

        @pl.when(counts_ref[j] == 2)
        def _():
            kx[2 * j + 1] = swap(keys.astype(F32)).astype(BF16)
            qx[2 * j + 1] = jnp.where(low, swap(q.astype(F32)), 0.0).astype(BF16)
            vx[2 * j + 1] = values(1)

    def plan(p, t):
        base = p * LIST
        end = base
        for j in range(BANDS):
            seen = jnp.where(jnp.logical_and(window_ref[p, j] == 1, p != j), 1, 0)
            keys_list[end] = 2 * j
            end = end + seen
            keys_list[end] = 2 * j + 1
            end = end + seen * (counts_ref[j] - 1)
        for u in range(STEP - 1):
            keys_list[end + u] = 0
        n = end - base
        chunks = (n + STEP - 1) // STEP

        def row(r, t):
            def chunk(c, t):
                step_q[t] = 2 * p + r
                step_k[t] = base + STEP * c
                step_left[t] = n - STEP * c
                step_flag[t] = jnp.where(c == 0, 1, 0) + jnp.where(c == chunks - 1, 2, 0)
                return t + 1

            return lax.fori_loop(0, chunks, chunk, t)

        return lax.fori_loop(0, counts_ref[p], row, t)

    def score(t, slot, u):
        s = lax.dot_general(
            kx[keys_list[step_k[t] + u]], qx[step_q[t]], (((1,), (1,)), ((), ())), preferred_element_type=F32
        )
        if u > 0:
            s = s + jnp.where(u < step_left[t], 0.0, NEG)
        s_ref[slot, u * COLS : (u + 1) * COLS] = s
        return jnp.max(s.reshape(COLS // 8, 8, COLS), axis=0)

    def keep_top(slot, tops):
        top = tops[0]
        for other in tops[1:]:
            top = jnp.maximum(top, other)
        top_ref[slot] = jnp.max(top, axis=0, keepdims=True)

    def scores(t, slot):
        keep_top(slot, [score(t, slot, u) for u in range(STEP)])

    def weigh(t, slot, later, later_slot):
        flag = step_flag[t]
        fresh = lax.rem(flag, 2) == 1
        old = jnp.where(fresh, NEG, best_ref[...])
        best = jnp.maximum(old, top_ref[slot])
        best_ref[...] = best
        acc = acc_ref[...] * jnp.where(fresh, 0.0, jnp.exp2(old - best))
        tops = []
        for u in range(STEP):
            w = jnp.exp2(s_ref[slot, u * COLS : (u + 1) * COLS] - best).astype(BF16)
            tops.append(score(later, later_slot, u))
            acc = acc + jnp.dot(vx[keys_list[step_k[t] + u]], w, preferred_element_type=F32)
        acc_ref[...] = acc
        keep_top(later_slot, tops)
        return acc, best, flag, step_q[t]

    def finish(acc, best, flag, qi):
        @pl.when(flag >= 2)
        def _():
            p, r = qi // 2, lax.rem(qi, 2)
            total = acc[HEAD_DIM : HEAD_DIM + 1]
            here = pl.ds(pl.multiple_of(r * HEAD_DIM, HEAD_DIM), HEAD_DIM)
            o_ref[p, here] = (acc[0:HEAD_DIM] / total).astype(BF16)
            lse_ref[p, pl.ds(r, 1)] = best + jnp.log2(total)

    @pl.when(mine)
    def _():
        copies = (
            pltpu.make_async_copy(q_hbm, q_ref, local_sem.at[0]),
            pltpu.make_async_copy(kv_hbm, kv_ref, local_sem.at[1]),
        )
        for c in copies:
            c.start()
        o_ref[...] = jnp.zeros_like(o_ref)
        lse_ref[...] = jnp.full(lse_ref.shape, NEG, F32)
        acc_ref[...] = jnp.zeros_like(acc_ref)
        best_ref[...] = jnp.full(best_ref.shape, NEG, F32)

        steps = lax.fori_loop(0, BANDS, plan, jnp.int32(0))
        for u in range(4 * AHEAD):
            step_q[steps + u] = 0
            step_k[steps + u] = 0
            step_left[steps + u] = 0
            step_flag[steps + u] = 0

        for c in copies:
            c.wait()

        @pl.loop(0, BANDS)
        def _(j):
            unpack(j)

        @pl.when(steps > 0)
        def _():
            for g in range(AHEAD):
                scores(g, g)

            @pl.loop(0, (steps + 2 * AHEAD - 1) // (2 * AHEAD))
            def _(i):
                for half in range(2):
                    now, then = half * AHEAD, (1 - half) * AHEAD
                    t = 2 * AHEAD * i + now
                    done = [weigh(t + g, now + g, t + AHEAD + g, then + g) for g in range(AHEAD)]
                    for d in done:
                        finish(*d)


def tail(
    counts_ref, o_hbm, lse_hbm, resid_hbm, own_hbm, own_lse_ref, out_hbm, mixed_ref,
    wout, o_in, lse_in, resid, own, att, sums,
    local_sem, o_send, o_recv, l_send, l_recv,
):
    me = lax.axis_index("patch")
    barrier = meet(me)
    copies = [
        pltpu.make_async_copy(s, d, local_sem.at[0]) for s, d in ((out_hbm, wout), (resid_hbm, resid), (own_hbm, own))
    ]
    for c in copies:
        c.start()
    pl.semaphore_wait(barrier, BANDS - 1)

    def heads_home(h):
        def far(i):
            to = lax.rem(me + i, BANDS)
            return (
                remote(o_hbm.at[to], o_in.at[h], o_send.at[to], o_recv.at[h], to),
                remote(lse_hbm.at[to], lse_in.at[h], l_send.at[to], l_recv.at[h], to),
            )

        def near():
            return (
                pltpu.make_async_copy(o_hbm.at[me], o_in.at[h], local_sem.at[1]),
                pltpu.make_async_copy(lse_hbm.at[me], lse_in.at[h], local_sem.at[1]),
            )

        return far, near

    for h in range(HEADS):
        @pl.when(owner(h) == me)
        def _():
            far, near = heads_home(h)

            @pl.loop(1, BANDS)
            def _(i):
                for c in far(i):
                    c.start()

            for c in near():
                c.start()

    for c in copies:
        c.wait()

    def arrived(h):
        @pl.when(owner(h) != me)
        def _():
            frm = owner(h)
            remote(o_hbm.at[0], o_in.at[h], o_send.at[0], o_recv.at[h], frm).wait_recv()
            remote(lse_hbm.at[0], lse_in.at[h], l_send.at[0], l_recv.at[h], frm).wait_recv()

        @pl.when(owner(h) == me)
        def _():
            for c in heads_home(h)[1]():
                c.wait()

    for first, last in ((0, 4), (4, 8), (8, HEADS)):
        for h in range(first, last):
            arrived(h)
        for h in range(first, last):
            chans = slice(h * HEAD_DIM, (h + 1) * HEAD_DIM)
            share = 1.0 / (1.0 + jnp.exp2(own_lse_ref[h] - lse_in[h]))
            for r in range(2):
                here = slice(r * COLS, (r + 1) * COLS)
                mine = own[chans, here].astype(F32)
                theirs = o_in[h, r * HEAD_DIM : (r + 1) * HEAD_DIM].astype(F32)
                att[chans, here] = (mine + (theirs - mine) * share[r : r + 1]).astype(BF16)
        chans = slice(first * HEAD_DIM, last * HEAD_DIM)
        for r in range(2):
            here = slice(r * COLS, (r + 1) * COLS)
            total = resid[here].astype(F32) if first == 0 else sums[here]
            total = total + lax.dot_general(
                att[chans, here], wout[chans], (((0,), (0,)), ((), ())), preferred_element_type=F32
            )
            if last < HEADS:
                sums[here] = total
                continue
            if r == 1:
                total = jnp.where(jnp.full(total.shape, counts_ref[me], jnp.int32) == 2, total, 0.0)
            mixed_ref[r] = total.astype(BF16)

    for h in range(HEADS):
        @pl.when(owner(h) == me)
        def _():
            far = heads_home(h)[0]

            @pl.loop(1, BANDS)
            def _(i):
                for c in far(i):
                    c.wait_send()


def body(
    latent, stale_kv, row_counts, window, time_index, norm_gain, conv_weight, time_first, time_second, attn_gain,
    attn_in, attn_out,
):
    smem = pl.BlockSpec(memory_space=pltpu.SMEM)
    vmem = pl.BlockSpec(memory_space=pltpu.VMEM)
    hbm = pl.BlockSpec(memory_space=pl.ANY)
    dma = pltpu.SemaphoreType.DMA
    shape = jax.ShapeDtypeStruct
    group = np.arange(CHANS) // (CHANS // GROUPS)
    gmat = jnp.asarray(group[:, None] == group[None, :], BF16)
    kv_all, q_all, resid, own, own_lse = pl.pallas_call(
        lead,
        out_shape=(
            shape((BANDS, TOK, 128), BF16),
            shape((BANDS, COLS, 128), BF16),
            shape((TOK, CHANS), BF16),
            shape((CHANS, TOK), BF16),
            shape((HEADS, 2, COLS), F32),
        ),
        in_specs=[smem, smem, vmem, vmem, vmem] + [hbm] * 6,
        out_specs=(hbm, hbm, vmem, vmem, vmem),
        scratch_shapes=[
            pltpu.VMEM((TOK, 2 * CHANS), BF16),
            pltpu.VMEM((3 * CHANS, 3 * CHANS), BF16),
            pltpu.VMEM(time_first.shape, BF16),
            pltpu.VMEM(time_second.shape, BF16),
            pltpu.VMEM((CHANS, 3 * CHANS), BF16),
            pltpu.VMEM((CHANS, CHANS), BF16),
            pltpu.VMEM((COLS, CHANS), BF16),
            pltpu.VMEM((2, COLS, CHANS), BF16),
            pltpu.VMEM((2, 2, CHANS), F32),
            pltpu.VMEM((2, BANDS, 2, CHANS), F32),
            pltpu.VMEM((TOK, CHANS), BF16),
            pltpu.VMEM((TOK, 3 * CHANS), F32),
            pltpu.VMEM((HEADS, TOK, 128), BF16),
            pltpu.VMEM((HEADS, COLS, 128), BF16),
            pltpu.VMEM((HEADS, TOK, 128), BF16),
            pltpu.VMEM((TOK, CHANS), BF16),
            pltpu.VMEM((CHANS, TOK), BF16),
            dma((7,)),
            dma((2, BANDS)),
            dma((2, BANDS)),
            dma((2,)),
            dma((2,)),
            dma((HEADS,)),
            dma((BANDS,)),
            dma((HEADS,)),
            dma((BANDS,)),
        ],
        compiler_params=pltpu.CompilerParams(
            collective_id=0, has_side_effects=True, vmem_limit_bytes=56 << 20
        ),
        name="lead",
    )(
        row_counts, time_index, latent, norm_gain, attn_gain, stale_kv,
        conv_weight, time_first, time_second, attn_in, gmat,
    )
    number = pltpu.SMEM((256,), jnp.int32)
    o_all, lse_all = pl.pallas_call(
        attend,
        out_shape=(shape((BANDS, 2 * HEAD_DIM, COLS), BF16), shape((BANDS, 2, COLS), F32)),
        in_specs=[smem, smem, hbm, hbm],
        out_specs=(vmem, vmem),
        scratch_shapes=[
            pltpu.VMEM((BANDS, COLS, 128), BF16),
            pltpu.VMEM((BANDS, TOK, 128), BF16),
            dma((2,)),
            pltpu.SMEM((BANDS * LIST + 8,), jnp.int32),
            number,
            number,
            number,
            number,
            pltpu.VMEM((2 * BANDS, COLS, 128), BF16),
            pltpu.VMEM((2 * BANDS, COLS, 128), BF16),
            pltpu.VMEM((2 * BANDS, HEAD_DIM + 16, COLS), BF16),
            pltpu.VMEM((2 * AHEAD, STEP * COLS, COLS), F32),
            pltpu.VMEM((2 * AHEAD, 1, COLS), F32),
            pltpu.VMEM((1, COLS), F32),
            pltpu.VMEM((HEAD_DIM + 16, COLS), F32),
        ],
        compiler_params=pltpu.CompilerParams(vmem_limit_bytes=56 << 20),
        name="attend",
    )(row_counts, window, q_all, kv_all)
    return pl.pallas_call(
        tail,
        out_shape=shape((2, COLS, CHANS), BF16),
        in_specs=[smem, hbm, hbm, hbm, hbm, vmem, hbm],
        out_specs=vmem,
        scratch_shapes=[
            pltpu.VMEM((CHANS, CHANS), BF16),
            pltpu.VMEM((HEADS, 2 * HEAD_DIM, COLS), BF16),
            pltpu.VMEM((HEADS, 2, COLS), F32),
            pltpu.VMEM((TOK, CHANS), BF16),
            pltpu.VMEM((CHANS, TOK), BF16),
            pltpu.VMEM((CHANS, TOK), BF16),
            pltpu.VMEM((TOK, CHANS), F32),
            dma((2,)),
            dma((BANDS,)),
            dma((HEADS,)),
            dma((BANDS,)),
            dma((HEADS,)),
        ],
        compiler_params=pltpu.CompilerParams(
            collective_id=1, has_side_effects=True, vmem_limit_bytes=56 << 20
        ),
        name="tail",
    )(row_counts, o_all, lse_all, resid, own, own_lse, attn_out)


def solution(mesh):
    part = P(("batch", "patch"))
    placed = (part, part, P("batch"), P("batch"), P("batch")) + (P(),) * 7
    return jax.shard_map(body, mesh=mesh, in_specs=placed, out_specs=part, check_vma=False)
```

```python
import math

import jax
import jax.numpy as jnp
import numpy as np
from jax import lax
from jax.experimental import pallas as pl
from jax.experimental.pallas import tpu as pltpu
from jax.sharding import PartitionSpec as P

HEAD_DIM = 64
GROUPS = 32
HEADS = 10
BANDS = 16
COLS = 256
CHANS = 640
TOK = 512
EPS = 1e-05
NEG = -1e30
MESH = pl.DeviceIdType.MESH
F32, BF16 = jnp.float32, jnp.bfloat16

OWNERS = ((0, 5, 10, 15, 1, 4, 11, 14, 3, 12), (0, 5, 10, 15, 2, 7, 8, 13, 6, 9))


def owner(head):
    core = lax.rem(lax.axis_index("batch"), 2)
    return OWNERS[0][head] + core * (OWNERS[1][head] - OWNERS[0][head])


def meet(me):
    barrier = pltpu.get_barrier_semaphore()

    @pl.loop(1, BANDS)
    def _(i):
        pl.semaphore_signal(
            barrier, inc=1, device_id={"patch": lax.rem(me + i, BANDS)}, device_id_type=MESH
        )

    return barrier


def remote(src, dst, send, recv, to):
    return pltpu.make_async_remote_copy(
        src, dst, send, recv, device_id={"patch": to}, device_id_type=MESH
    )


def lanes(shape):
    return lax.broadcasted_iota(jnp.int32, shape, 1)


def swap(x):
    return pltpu.roll(x, HEAD_DIM, 1)


def group_sum(vec, gmat):
    hi = vec.astype(BF16)
    rest = vec - hi.astype(F32)
    mid = rest.astype(BF16)
    low = (rest - mid.astype(F32)).astype(BF16)
    row = lax.broadcasted_iota(jnp.int32, (16, CHANS), 0)
    stack = jnp.where(
        row == 0,
        hi.astype(F32),
        jnp.where(row == 1, mid.astype(F32), jnp.where(row == 2, low.astype(F32), 0.0)),
    ).astype(BF16)
    out = jnp.dot(stack, gmat, preferred_element_type=F32)
    return jnp.sum(out, axis=0, keepdims=True)


def local_stats(x0, x1, live1, out_ref):
    tok = COLS * (1.0 + live1)
    sums = jnp.sum(x0, axis=0, keepdims=True) + live1 * jnp.sum(x1, axis=0, keepdims=True)
    mean = sums / tok
    d0, d1 = x0 - mean, x1 - mean
    spread = jnp.sum(d0 * d0, axis=0, keepdims=True) + live1 * jnp.sum(d1 * d1, axis=0, keepdims=True)
    out_ref[0:1, :] = sums
    out_ref[1:2, :] = spread


def merge_stats(stats_ref, counts_ref, gain, gmat):
    total = jnp.zeros((1, CHANS), F32)
    rows = 0
    for b in range(BANDS):
        total = total + stats_ref[b, 0:1, :]
        rows = rows + counts_ref[b]
    count = rows.astype(F32) * (COLS * (CHANS // GROUPS))
    mean = group_sum(total, gmat) / count
    spread = jnp.zeros((1, CHANS), F32)
    for b in range(BANDS):
        tok = counts_ref[b].astype(F32) * COLS
        off = stats_ref[b, 0:1, :] / tok - mean
        spread = spread + stats_ref[b, 1:2, :] + tok * (off * off)
    var = group_sum(spread, gmat) / count
    return mean, 0.5 * lax.rsqrt(var + EPS) * gain


def norm(x, mean, half):
    y = (x - mean) * half
    return y + y * jnp.tanh(y)


def side_by_side(x):
    turned = swap(x)
    low = lanes((COLS, 128)) < HEAD_DIM
    return jnp.where(low, x[0:COLS], turned[COLS:TOK]), jnp.where(low, turned[0:COLS], x[COLS:TOK])


def lead(
    counts_ref, time_ref, latent_hbm, gain1_ref, gain2_ref, stale_hbm, conv_hbm, first_hbm, second_hbm, in_hbm, gmat_hbm,
    kv_all, q_all, resid_ref, own_ref, lse_ref,
    latent_ref, stale, wcat, wfirst, wsecond, win, gmat, halo_out, halo_in, stats_out, stats_in, x_ref, y_ref,
    kvp, qp, qs, kf, vt,
    local_sem, stat_send, stat_recv, halo_send, halo_recv, kv_send, kv_recv, q_send, q_recv,
):
    me = lax.axis_index("patch")
    up, down = lax.rem(me + 1, BANDS), lax.rem(me + BANDS - 1, BANDS)
    barrier = meet(me)

    copies = {
        "latent": [(latent_hbm, latent_ref)],
        "stale": [(stale_hbm, stale)],
        "gmat": [(gmat_hbm, gmat)],
        "time": [(first_hbm, wfirst), (second_hbm, wsecond)],
        "conv": [
            (conv_hbm.at[dy, dx], wcat.at[pl.ds(dy * CHANS, CHANS), pl.ds(dx * CHANS, CHANS)])
            for dy in range(3)
            for dx in range(3)
        ],
        "in": [(in_hbm, win)],
    }
    copies = {
        name: [pltpu.make_async_copy(s, d, local_sem.at[i]) for s, d in pairs]
        for i, (name, pairs) in enumerate(copies.items())
    }
    for group in copies.values():
        for c in group:
            c.start()

    def arrived(name):
        for c in copies[name]:
            c.wait()

    mine = counts_ref[me]
    live1 = (mine - 1).astype(F32)
    two = jnp.full((COLS, CHANS), mine, jnp.int32) == 2

    arrived("latent")
    halo_out[...] = jnp.where(two, latent_ref[1], latent_ref[0])
    local_stats(latent_ref[0].astype(F32), latent_ref[1].astype(F32), live1, stats_out.at[0])
    stats_in[0, me] = stats_out[0]

    pl.semaphore_wait(barrier, BANDS - 1)

    def send_stats(turn):
        @pl.loop(1, BANDS)
        def _(i):
            to = lax.rem(me + i, BANDS)
            remote(
                stats_out.at[turn], stats_in.at[turn, me], stat_send.at[turn, to], stat_recv.at[turn, me], to
            ).start()

    def wait_stats(turn):
        @pl.loop(1, BANDS)
        def _(i):
            to = lax.rem(me + i, BANDS)
            c = remote(
                stats_out.at[turn], stats_in.at[turn, to], stat_send.at[turn, to], stat_recv.at[turn, to], to
            )
            c.wait_send()
            c.wait_recv()

    halos = (
        remote(halo_out, halo_in.at[0], halo_send.at[0], halo_recv.at[0], up),
        remote(latent_ref.at[0], halo_in.at[1], halo_send.at[1], halo_recv.at[1], down),
    )
    send_stats(0)
    for c in halos:
        c.start()

    arrived("stale")

    @pl.loop(0, HEADS // 2)
    def _(i):
        at = pl.multiple_of(i * 128, 128)
        keys = side_by_side(stale[:, pl.ds(at, 128)].astype(F32))
        vals = stale[:, pl.ds(pl.multiple_of(CHANS + i * 128, 128), 128)].astype(F32).T
        for sub in range(2):
            h = 2 * i + sub
            kvp[h, 0:COLS] = keys[sub].astype(BF16)
            for blk in range(4):
                kvp[h, COLS + blk * HEAD_DIM : COLS + (blk + 1) * HEAD_DIM] = vals[
                    sub * HEAD_DIM : (sub + 1) * HEAD_DIM, blk * 128 : (blk + 1) * 128
                ].astype(BF16)

    def to_owners(src, dst, send, recv, local):
        def far(h):
            return remote(src.at[h], dst.at[me], send.at[h], recv.at[me], owner(h))

        def near(h):
            return pltpu.make_async_copy(src.at[h], dst.at[me], local)

        def send_to(i):
            to = lax.rem(me + i, BANDS)
            head, found = jnp.int32(0), jnp.int32(0)
            for h in range(HEADS):
                hit = jnp.where(owner(h) == to, 1, 0)
                head, found = head + h * hit, found + hit

            @pl.when(found == 1)
            def _():
                remote(src.at[head], dst.at[me], send.at[head], recv.at[me], to).start()

        def start_column():
            for i in (4, 8, 12):
                send_to(i)
            for h in range(HEADS):
                @pl.when(owner(h) == me)
                def _():
                    near(h).start()

        def start_rest():
            @pl.loop(1, BANDS)
            def _(i):
                @pl.when(lax.rem(i, 4) != 0)
                def _():
                    send_to(i)

        def wait():
            for h in range(HEADS):
                @pl.when(owner(h) != me)
                def _():
                    far(h).wait_send()

                @pl.when(owner(h) == me)
                def _():
                    near(h).wait()

                    @pl.loop(1, BANDS)
                    def _(i):
                        frm = lax.rem(me + i, BANDS)
                        remote(src.at[h], dst.at[frm], send.at[h], recv.at[frm], frm).wait_recv()

        return start_column, start_rest, wait

    column_kv, rest_kv, wait_kv = to_owners(kvp, kv_all, kv_send, kv_recv, local_sem.at[6])
    column_q, rest_q, wait_q = to_owners(qp, q_all, q_send, q_recv, local_sem.at[7])

    column_kv()

    arrived("time")
    half = wfirst.shape[0] // 2
    lane = lanes((8, 2 * half))
    k = jnp.where(lane < half, lane, lane - half).astype(F32)
    angles = time_ref[0].astype(F32) * jnp.exp(-math.log(10000.0) * k / half)
    sinus = jnp.where(lane < half, jnp.cos(angles), jnp.sin(angles)).astype(BF16)
    hidden = jnp.dot(sinus, wfirst[...], preferred_element_type=F32)
    hidden = (hidden / (1.0 + jnp.exp(-hidden))).astype(BF16)
    tvec = jnp.dot(hidden, wsecond[...], preferred_element_type=F32)[0:1, :]

    arrived("gmat")
    wait_stats(0)
    mean, scale = merge_stats(stats_in.at[0], counts_ref, gain1_ref[...].astype(F32)[None], gmat[...])
    x_ref[0:COLS] = norm(latent_ref[0].astype(F32), mean, scale).astype(BF16)
    x_ref[COLS:TOK] = jnp.where(two, norm(latent_ref[1].astype(F32), mean, scale), 0.0).astype(BF16)

    arrived("conv")
    chunk = 256
    whole = 3 * CHANS // chunk

    def each_chunk(step):
        @pl.loop(0, whole)
        def _(i):
            step(pl.ds(pl.multiple_of(i * chunk, chunk), chunk))

        step(slice(whole * chunk, 3 * CHANS))

    def own_rows(at):
        mid = jnp.dot(x_ref[...], wcat[CHANS : 2 * CHANS, at], preferred_element_type=F32)
        under = jnp.dot(x_ref[COLS:TOK], wcat[2 * CHANS :, at], preferred_element_type=F32)
        over = jnp.dot(x_ref[0:COLS], wcat[0:CHANS, at], preferred_element_type=F32)
        y_ref[0:COLS, at] = mid[0:COLS] + under
        y_ref[COLS:TOK, at] = mid[COLS:TOK] + over

    each_chunk(own_rows)
    for c in halos:
        c.wait()
    rest_kv()
    x_ref[0:COLS] = jnp.where(
        jnp.full((COLS, CHANS), me, jnp.int32) > 0, norm(halo_in[0].astype(F32), mean, scale), 0.0
    ).astype(BF16)
    x_ref[COLS:TOK] = jnp.where(
        jnp.full((COLS, CHANS), me, jnp.int32) < BANDS - 1, norm(halo_in[1].astype(F32), mean, scale), 0.0
    ).astype(BF16)

    def other_rows(at):
        over = jnp.dot(x_ref[0:COLS], wcat[0:CHANS, at], preferred_element_type=F32)
        under = jnp.dot(x_ref[COLS:TOK], wcat[2 * CHANS :, at], preferred_element_type=F32)
        both = jnp.full(under.shape, mine, jnp.int32) == 2
        y_ref[0:COLS, at] = y_ref[0:COLS, at] + over + jnp.where(both, 0.0, under)
        y_ref[COLS:TOK, at] = y_ref[COLS:TOK, at] + jnp.where(both, under, 0.0)

    each_chunk(other_rows)
    row = lax.broadcasted_iota(jnp.int32, (COLS, CHANS), 0)
    for r in range(2):
        here = slice(r * COLS, (r + 1) * COLS)
        left = pltpu.roll(y_ref[here, 0:CHANS], 1, 0)
        right = pltpu.roll(y_ref[here, 2 * CHANS :], COLS - 1, 0)
        conv = y_ref[here, CHANS : 2 * CHANS] + jnp.where(row == 0, 0.0, left) + jnp.where(
            row == COLS - 1, 0.0, right
        )
        resid_ref[here, :] = (latent_ref[r].astype(F32) + conv + tvec).astype(BF16)

    local_stats(resid_ref[0:COLS].astype(F32), resid_ref[COLS:TOK].astype(F32), live1, stats_out.at[1])
    stats_in[1, me] = stats_out[1]
    send_stats(1)
    arrived("in")
    wait_stats(1)
    mean, scale = merge_stats(stats_in.at[1], counts_ref, gain2_ref[...].astype(F32)[None], gmat[...])
    x_ref[0:COLS] = norm(resid_ref[0:COLS].astype(F32), mean, scale).astype(BF16)
    x_ref[COLS:TOK] = jnp.where(two, norm(resid_ref[COLS:TOK].astype(F32), mean, scale), 0.0).astype(BF16)

    fold = HEAD_DIM**-0.5 * math.log2(math.e)
    query = jnp.dot(x_ref[...], win[:, 0:CHANS], preferred_element_type=F32) * fold
    low = lanes((TOK, 128)) < HEAD_DIM
    for i in range(HEADS // 2):
        pair = query[:, i * 128 : (i + 1) * 128]
        qs[2 * i] = jnp.where(low, pair, 0.0).astype(BF16)
        qs[2 * i + 1] = jnp.where(low, 0.0, pair).astype(BF16)
        for sub, packed in enumerate(side_by_side(pair)):
            qp[2 * i + sub] = packed.astype(BF16)
    rest_q()
    column_q()

    kf[...] = jnp.dot(x_ref[...], win[:, CHANS : 2 * CHANS], preferred_element_type=F32).astype(BF16)
    vals = jnp.dot(x_ref[...], win[:, 2 * CHANS :], preferred_element_type=F32)
    for i in range(HEADS // 2):
        vt[i * 128 : (i + 1) * 128] = vals[:, i * 128 : (i + 1) * 128].T.astype(BF16)
    shut = jnp.where(mine == 2, 0.0, NEG)
    ones = jnp.ones((16, TOK), BF16)

    @pl.loop(0, HEADS // 2)
    def _(i):
        keys = kf[:, pl.ds(pl.multiple_of(i * 128, 128), 128)]
        for sub in range(2):
            h = 2 * i + sub
            chans = pl.ds(pl.multiple_of(h * HEAD_DIM, HEAD_DIM), HEAD_DIM)
            values = jnp.concatenate([vt[chans], ones], axis=0)
            for r in range(2):
                here = slice(r * COLS, (r + 1) * COLS)
                s = lax.dot_general(
                    keys, qs[h, here], (((1,), (1,)), ((), ())), preferred_element_type=F32
                )
                s0, s1 = s[0:COLS], s[COLS:TOK] + shut
                best = jnp.max(jnp.maximum(s0, s1), axis=0, keepdims=True)
                w = jnp.concatenate([jnp.exp2(s0 - best), jnp.exp2(s1 - best)], axis=0).astype(BF16)
                acc = jnp.dot(values, w, preferred_element_type=F32)
                total = acc[HEAD_DIM : HEAD_DIM + 1]
                own_ref[chans, here] = (acc[0:HEAD_DIM] / total).astype(BF16)
                lse_ref[h, r : r + 1, :] = best + jnp.log2(total)

    wait_kv()
    wait_q()


STEP = 4
AHEAD = 4
LIST = 24


def attend(
    counts_ref, window_ref, q_hbm, kv_hbm, o_ref, lse_ref,
    q_ref, kv_ref, local_sem, keys_list, step_q, step_k, step_left, step_flag, kx, qx, vx, s_ref, top_ref, best_ref, acc_ref,
):
    me = lax.axis_index("patch")
    mine = owner(0) == me
    for h in range(1, HEADS):
        mine = jnp.logical_or(mine, owner(h) == me)
    low = lanes((COLS, 128)) < HEAD_DIM

    def unpack(j):
        ones = jnp.ones((16, COLS), BF16)

        def values(r):
            at = COLS + 2 * r * HEAD_DIM
            pair = [kv_ref[j, at : at + HEAD_DIM], kv_ref[j, at + HEAD_DIM : at + 2 * HEAD_DIM]]
            return jnp.concatenate([jnp.concatenate(pair, axis=1), ones], axis=0)

        keys, q = kv_ref[j, 0:COLS], q_ref[j]
        kx[2 * j] = keys
        qx[2 * j] = jnp.where(low, q, jnp.zeros_like(q))
        vx[2 * j] = values(0)

        @pl.when(counts_ref[j] == 2)
        def _():
            kx[2 * j + 1] = swap(keys.astype(F32)).astype(BF16)
            qx[2 * j + 1] = jnp.where(low, swap(q.astype(F32)), 0.0).astype(BF16)
            vx[2 * j + 1] = values(1)

    def plan(p, t):
        base = p * LIST
        end = base
        for j in range(BANDS):
            seen = jnp.where(jnp.logical_and(window_ref[p, j] == 1, p != j), 1, 0)
            keys_list[end] = 2 * j
            end = end + seen
            keys_list[end] = 2 * j + 1
            end = end + seen * (counts_ref[j] - 1)
        for u in range(STEP - 1):
            keys_list[end + u] = 0
        n = end - base
        chunks = (n + STEP - 1) // STEP

        def row(r, t):
            def chunk(c, t):
                step_q[t] = 2 * p + r
                step_k[t] = base + STEP * c
                step_left[t] = n - STEP * c
                step_flag[t] = jnp.where(c == 0, 1, 0) + jnp.where(c == chunks - 1, 2, 0)
                return t + 1

            return lax.fori_loop(0, chunks, chunk, t)

        return lax.fori_loop(0, counts_ref[p], row, t)

    def score(t, slot, u):
        s = lax.dot_general(
            kx[keys_list[step_k[t] + u]], qx[step_q[t]], (((1,), (1,)), ((), ())), preferred_element_type=F32
        )
        if u > 0:
            s = s + jnp.where(u < step_left[t], 0.0, NEG)
        s_ref[slot, u * COLS : (u + 1) * COLS] = s
        return jnp.max(s.reshape(COLS // 8, 8, COLS), axis=0)

    def keep_top(slot, tops):
        top = tops[0]
        for other in tops[1:]:
            top = jnp.maximum(top, other)
        top_ref[slot] = jnp.max(top, axis=0, keepdims=True)

    def scores(t, slot):
        keep_top(slot, [score(t, slot, u) for u in range(STEP)])

    def weigh(t, slot, later, later_slot):
        flag = step_flag[t]
        fresh = lax.rem(flag, 2) == 1
        old = jnp.where(fresh, NEG, best_ref[...])
        best = jnp.maximum(old, top_ref[slot])
        best_ref[...] = best
        acc = acc_ref[...] * jnp.where(fresh, 0.0, jnp.exp2(old - best))
        tops = []
        for u in range(STEP):
            w = jnp.exp2(s_ref[slot, u * COLS : (u + 1) * COLS] - best).astype(BF16)
            tops.append(score(later, later_slot, u))
            acc = acc + jnp.dot(vx[keys_list[step_k[t] + u]], w, preferred_element_type=F32)
        acc_ref[...] = acc
        keep_top(later_slot, tops)
        return acc, best, flag, step_q[t]

    def finish(acc, best, flag, qi):
        @pl.when(flag >= 2)
        def _():
            p, r = qi // 2, lax.rem(qi, 2)
            total = acc[HEAD_DIM : HEAD_DIM + 1]
            here = pl.ds(pl.multiple_of(r * HEAD_DIM, HEAD_DIM), HEAD_DIM)
            o_ref[p, here] = (acc[0:HEAD_DIM] / total).astype(BF16)
            lse_ref[p, pl.ds(r, 1)] = best + jnp.log2(total)

    @pl.when(mine)
    def _():
        copies = (
            pltpu.make_async_copy(q_hbm, q_ref, local_sem.at[0]),
            pltpu.make_async_copy(kv_hbm, kv_ref, local_sem.at[1]),
        )
        for c in copies:
            c.start()
        o_ref[...] = jnp.zeros_like(o_ref)
        lse_ref[...] = jnp.full(lse_ref.shape, NEG, F32)
        acc_ref[...] = jnp.zeros_like(acc_ref)
        best_ref[...] = jnp.full(best_ref.shape, NEG, F32)

        steps = lax.fori_loop(0, BANDS, plan, jnp.int32(0))
        for u in range(4 * AHEAD):
            step_q[steps + u] = 0
            step_k[steps + u] = 0
            step_left[steps + u] = 0
            step_flag[steps + u] = 0

        for c in copies:
            c.wait()

        @pl.loop(0, BANDS)
        def _(j):
            unpack(j)

        @pl.when(steps > 0)
        def _():
            for g in range(AHEAD):
                scores(g, g)

            @pl.loop(0, (steps + 2 * AHEAD - 1) // (2 * AHEAD))
            def _(i):
                for half in range(2):
                    now, then = half * AHEAD, (1 - half) * AHEAD
                    t = 2 * AHEAD * i + now
                    done = [weigh(t + g, now + g, t + AHEAD + g, then + g) for g in range(AHEAD)]
                    for d in done:
                        finish(*d)


def tail(
    counts_ref, o_hbm, lse_hbm, resid_hbm, own_hbm, own_lse_ref, out_hbm, mixed_ref,
    wout, o_in, lse_in, resid, own, att, sums,
    local_sem, o_send, o_recv, l_send, l_recv,
):
    me = lax.axis_index("patch")
    barrier = meet(me)
    copies = [
        pltpu.make_async_copy(s, d, local_sem.at[0]) for s, d in ((out_hbm, wout), (resid_hbm, resid), (own_hbm, own))
    ]
    for c in copies:
        c.start()
    pl.semaphore_wait(barrier, BANDS - 1)

    def heads_home(h):
        def far(i):
            to = lax.rem(me + i, BANDS)
            return (
                remote(o_hbm.at[to], o_in.at[h], o_send.at[to], o_recv.at[h], to),
                remote(lse_hbm.at[to], lse_in.at[h], l_send.at[to], l_recv.at[h], to),
            )

        def near():
            return (
                pltpu.make_async_copy(o_hbm.at[me], o_in.at[h], local_sem.at[1]),
                pltpu.make_async_copy(lse_hbm.at[me], lse_in.at[h], local_sem.at[1]),
            )

        return far, near

    for h in range(HEADS):
        @pl.when(owner(h) == me)
        def _():
            far, near = heads_home(h)

            @pl.loop(1, BANDS)
            def _(i):
                for c in far(i):
                    c.start()

            for c in near():
                c.start()

    for c in copies:
        c.wait()

    def arrived(h):
        @pl.when(owner(h) != me)
        def _():
            frm = owner(h)
            remote(o_hbm.at[0], o_in.at[h], o_send.at[0], o_recv.at[h], frm).wait_recv()
            remote(lse_hbm.at[0], lse_in.at[h], l_send.at[0], l_recv.at[h], frm).wait_recv()

        @pl.when(owner(h) == me)
        def _():
            for c in heads_home(h)[1]():
                c.wait()

    for first, last in ((0, 4), (4, 8), (8, HEADS)):
        for h in range(first, last):
            arrived(h)
        for h in range(first, last):
            chans = slice(h * HEAD_DIM, (h + 1) * HEAD_DIM)
            share = 1.0 / (1.0 + jnp.exp2(own_lse_ref[h] - lse_in[h]))
            for r in range(2):
                here = slice(r * COLS, (r + 1) * COLS)
                mine = own[chans, here].astype(F32)
                theirs = o_in[h, r * HEAD_DIM : (r + 1) * HEAD_DIM].astype(F32)
                att[chans, here] = (mine + (theirs - mine) * share[r : r + 1]).astype(BF16)
        chans = slice(first * HEAD_DIM, last * HEAD_DIM)
        for r in range(2):
            here = slice(r * COLS, (r + 1) * COLS)
            total = resid[here].astype(F32) if first == 0 else sums[here]
            total = total + lax.dot_general(
                att[chans, here], wout[chans], (((0,), (0,)), ((), ())), preferred_element_type=F32
            )
            if last < HEADS:
                sums[here] = total
                continue
            if r == 1:
                total = jnp.where(jnp.full(total.shape, counts_ref[me], jnp.int32) == 2, total, 0.0)
            mixed_ref[r] = total.astype(BF16)

    for h in range(HEADS):
        @pl.when(owner(h) == me)
        def _():
            far = heads_home(h)[0]

            @pl.loop(1, BANDS)
            def _(i):
                for c in far(i):
                    c.wait_send()


def body(
    latent, stale_kv, row_counts, window, time_index, norm_gain, conv_weight, time_first, time_second, attn_gain,
    attn_in, attn_out,
):
    smem = pl.BlockSpec(memory_space=pltpu.SMEM)
    vmem = pl.BlockSpec(memory_space=pltpu.VMEM)
    hbm = pl.BlockSpec(memory_space=pl.ANY)
    dma = pltpu.SemaphoreType.DMA
    shape = jax.ShapeDtypeStruct
    group = np.arange(CHANS) // (CHANS // GROUPS)
    gmat = jnp.asarray(group[:, None] == group[None, :], BF16)
    kv_all, q_all, resid, own, own_lse = pl.pallas_call(
        lead,
        out_shape=(
            shape((BANDS, TOK, 128), BF16),
            shape((BANDS, COLS, 128), BF16),
            shape((TOK, CHANS), BF16),
            shape((CHANS, TOK), BF16),
            shape((HEADS, 2, COLS), F32),
        ),
        in_specs=[smem, smem, hbm, vmem, vmem] + [hbm] * 6,
        out_specs=(hbm, hbm, vmem, vmem, vmem),
        scratch_shapes=[
            pltpu.VMEM((2, COLS, CHANS), BF16),
            pltpu.VMEM((TOK, 2 * CHANS), BF16),
            pltpu.VMEM((3 * CHANS, 3 * CHANS), BF16),
            pltpu.VMEM(time_first.shape, BF16),
            pltpu.VMEM(time_second.shape, BF16),
            pltpu.VMEM((CHANS, 3 * CHANS), BF16),
            pltpu.VMEM((CHANS, CHANS), BF16),
            pltpu.VMEM((COLS, CHANS), BF16),
            pltpu.VMEM((2, COLS, CHANS), BF16),
            pltpu.VMEM((2, 2, CHANS), F32),
            pltpu.VMEM((2, BANDS, 2, CHANS), F32),
            pltpu.VMEM((TOK, CHANS), BF16),
            pltpu.VMEM((TOK, 3 * CHANS), F32),
            pltpu.VMEM((HEADS, TOK, 128), BF16),
            pltpu.VMEM((HEADS, COLS, 128), BF16),
            pltpu.VMEM((HEADS, TOK, 128), BF16),
            pltpu.VMEM((TOK, CHANS), BF16),
            pltpu.VMEM((CHANS, TOK), BF16),
            dma((9,)),
            dma((2, BANDS)),
            dma((2, BANDS)),
            dma((2,)),
            dma((2,)),
            dma((HEADS,)),
            dma((BANDS,)),
            dma((HEADS,)),
            dma((BANDS,)),
        ],
        compiler_params=pltpu.CompilerParams(
            collective_id=0, has_side_effects=True, vmem_limit_bytes=56 << 20
        ),
        name="lead",
    )(
        row_counts, time_index, latent, norm_gain, attn_gain, stale_kv,
        conv_weight, time_first, time_second, attn_in, gmat,
    )
    number = pltpu.SMEM((256,), jnp.int32)
    o_all, lse_all = pl.pallas_call(
        attend,
        out_shape=(shape((BANDS, 2 * HEAD_DIM, COLS), BF16), shape((BANDS, 2, COLS), F32)),
        in_specs=[smem, smem, hbm, hbm],
        out_specs=(vmem, vmem),
        scratch_shapes=[
            pltpu.VMEM((BANDS, COLS, 128), BF16),
            pltpu.VMEM((BANDS, TOK, 128), BF16),
            dma((2,)),
            pltpu.SMEM((BANDS * LIST + 8,), jnp.int32),
            number,
            number,
            number,
            number,
            pltpu.VMEM((2 * BANDS, COLS, 128), BF16),
            pltpu.VMEM((2 * BANDS, COLS, 128), BF16),
            pltpu.VMEM((2 * BANDS, HEAD_DIM + 16, COLS), BF16),
            pltpu.VMEM((2 * AHEAD, STEP * COLS, COLS), F32),
            pltpu.VMEM((2 * AHEAD, 1, COLS), F32),
            pltpu.VMEM((1, COLS), F32),
            pltpu.VMEM((HEAD_DIM + 16, COLS), F32),
        ],
        compiler_params=pltpu.CompilerParams(vmem_limit_bytes=56 << 20),
        name="attend",
    )(row_counts, window, q_all, kv_all)
    return pl.pallas_call(
        tail,
        out_shape=shape((2, COLS, CHANS), BF16),
        in_specs=[smem, hbm, hbm, hbm, hbm, vmem, hbm],
        out_specs=vmem,
        scratch_shapes=[
            pltpu.VMEM((CHANS, CHANS), BF16),
            pltpu.VMEM((HEADS, 2 * HEAD_DIM, COLS), BF16),
            pltpu.VMEM((HEADS, 2, COLS), F32),
            pltpu.VMEM((TOK, CHANS), BF16),
            pltpu.VMEM((CHANS, TOK), BF16),
            pltpu.VMEM((CHANS, TOK), BF16),
            pltpu.VMEM((TOK, CHANS), F32),
            dma((2,)),
            dma((BANDS,)),
            dma((HEADS,)),
            dma((BANDS,)),
            dma((HEADS,)),
        ],
        compiler_params=pltpu.CompilerParams(
            collective_id=1, has_side_effects=True, vmem_limit_bytes=56 << 20
        ),
        name="tail",
    )(row_counts, o_all, lse_all, resid, own, own_lse, attn_out)


def solution(mesh):
    part = P(("batch", "patch"))
    placed = (part, part, P("batch"), P("batch"), P("batch")) + (P(),) * 7
    return jax.shard_map(body, mesh=mesh, in_specs=placed, out_specs=part, check_vma=False)
```

```python
import math

import jax
import jax.numpy as jnp
import numpy as np
from jax import lax
from jax.experimental import pallas as pl
from jax.experimental.pallas import tpu as pltpu
from jax.sharding import PartitionSpec as P

HEAD_DIM = 64
GROUPS = 32
HEADS = 10
BANDS = 16
COLS = 256
CHANS = 640
TOK = 512
EPS = 1e-05
NEG = -1e30
MESH = pl.DeviceIdType.MESH
F32, BF16 = jnp.float32, jnp.bfloat16

OWNERS = ((0, 5, 10, 15, 1, 4, 11, 14, 3, 12), (0, 5, 10, 15, 2, 7, 8, 13, 6, 9))


def owner(head):
    core = lax.rem(lax.axis_index("batch"), 2)
    return OWNERS[0][head] + core * (OWNERS[1][head] - OWNERS[0][head])


def meet(me):
    barrier = pltpu.get_barrier_semaphore()

    @pl.loop(1, BANDS)
    def _(i):
        pl.semaphore_signal(
            barrier, inc=1, device_id={"patch": lax.rem(me + i, BANDS)}, device_id_type=MESH
        )

    return barrier


def remote(src, dst, send, recv, to):
    return pltpu.make_async_remote_copy(
        src, dst, send, recv, device_id={"patch": to}, device_id_type=MESH
    )


def lanes(shape):
    return lax.broadcasted_iota(jnp.int32, shape, 1)


def swap(x):
    return pltpu.roll(x, HEAD_DIM, 1)


def group_sum(vec, gmat):
    hi = vec.astype(BF16)
    rest = vec - hi.astype(F32)
    mid = rest.astype(BF16)
    low = (rest - mid.astype(F32)).astype(BF16)
    row = lax.broadcasted_iota(jnp.int32, (16, CHANS), 0)
    stack = jnp.where(
        row == 0,
        hi.astype(F32),
        jnp.where(row == 1, mid.astype(F32), jnp.where(row == 2, low.astype(F32), 0.0)),
    ).astype(BF16)
    out = jnp.dot(stack, gmat, preferred_element_type=F32)
    return jnp.sum(out, axis=0, keepdims=True)


def local_stats(x0, x1, live1, out_ref):
    tok = COLS * (1.0 + live1)
    sums = jnp.sum(x0, axis=0, keepdims=True) + live1 * jnp.sum(x1, axis=0, keepdims=True)
    mean = sums / tok
    d0, d1 = x0 - mean, x1 - mean
    spread = jnp.sum(d0 * d0, axis=0, keepdims=True) + live1 * jnp.sum(d1 * d1, axis=0, keepdims=True)
    out_ref[0:1, :] = sums
    out_ref[1:2, :] = spread


def merge_stats(stats_ref, counts_ref, gain, gmat):
    total = jnp.zeros((1, CHANS), F32)
    rows = 0
    for b in range(BANDS):
        total = total + stats_ref[b, 0:1, :]
        rows = rows + counts_ref[b]
    count = rows.astype(F32) * (COLS * (CHANS // GROUPS))
    mean = group_sum(total, gmat) / count
    spread = jnp.zeros((1, CHANS), F32)
    for b in range(BANDS):
        tok = counts_ref[b].astype(F32) * COLS
        off = stats_ref[b, 0:1, :] / tok - mean
        spread = spread + stats_ref[b, 1:2, :] + tok * (off * off)
    var = group_sum(spread, gmat) / count
    return mean, 0.5 * lax.rsqrt(var + EPS) * gain


def norm(x, mean, half):
    y = (x - mean) * half
    return y + y * jnp.tanh(y)


def side_by_side(x):
    turned = swap(x)
    low = lanes((COLS, 128)) < HEAD_DIM
    return jnp.where(low, x[0:COLS], turned[COLS:TOK]), jnp.where(low, turned[0:COLS], x[COLS:TOK])


def lead(
    counts_ref, time_ref, latent_hbm, gain1_hbm, gain2_hbm, stale_hbm, conv_hbm, first_hbm, second_hbm, in_hbm, gmat_hbm,
    kv_all, q_all, resid_ref, own_ref, lse_ref,
    latent_ref, gain1_ref, gain2_ref, stale, wcat, wfirst, wsecond, win, gmat, halo_out, halo_in, stats_out, stats_in, x_ref, y_ref,
    kvp, qp, qs, kf, vt,
    local_sem, stat_send, stat_recv, halo_send, halo_recv, kv_send, kv_recv, q_send, q_recv,
):
    me = lax.axis_index("patch")
    up, down = lax.rem(me + 1, BANDS), lax.rem(me + BANDS - 1, BANDS)
    barrier = meet(me)

    copies = {
        "latent": [(latent_hbm, latent_ref)],
        "stale": [(stale_hbm, stale)],
        "gmat": [(gmat_hbm, gmat), (gain1_hbm, gain1_ref), (gain2_hbm, gain2_ref)],
        "time": [(first_hbm, wfirst), (second_hbm, wsecond)],
        "conv": [
            (conv_hbm.at[dy, dx], wcat.at[pl.ds(dy * CHANS, CHANS), pl.ds(dx * CHANS, CHANS)])
            for dy in range(3)
            for dx in range(3)
        ],
        "in": [(in_hbm, win)],
    }
    copies = {
        name: [pltpu.make_async_copy(s, d, local_sem.at[i]) for s, d in pairs]
        for i, (name, pairs) in enumerate(copies.items())
    }
    for group in copies.values():
        for c in group:
            c.start()

    def arrived(name):
        for c in copies[name]:
            c.wait()

    mine = counts_ref[me]
    live1 = (mine - 1).astype(F32)
    two = jnp.full((COLS, CHANS), mine, jnp.int32) == 2

    arrived("latent")
    halo_out[...] = jnp.where(two, latent_ref[1], latent_ref[0])
    local_stats(latent_ref[0].astype(F32), latent_ref[1].astype(F32), live1, stats_out.at[0])
    stats_in[0, me] = stats_out[0]

    pl.semaphore_wait(barrier, BANDS - 1)

    def send_stats(turn):
        @pl.loop(1, BANDS)
        def _(i):
            to = lax.rem(me + i, BANDS)
            remote(
                stats_out.at[turn], stats_in.at[turn, me], stat_send.at[turn, to], stat_recv.at[turn, me], to
            ).start()

    def wait_stats(turn):
        @pl.loop(1, BANDS)
        def _(i):
            to = lax.rem(me + i, BANDS)
            c = remote(
                stats_out.at[turn], stats_in.at[turn, to], stat_send.at[turn, to], stat_recv.at[turn, to], to
            )
            c.wait_send()
            c.wait_recv()

    halos = (
        remote(halo_out, halo_in.at[0], halo_send.at[0], halo_recv.at[0], up),
        remote(latent_ref.at[0], halo_in.at[1], halo_send.at[1], halo_recv.at[1], down),
    )
    send_stats(0)
    for c in halos:
        c.start()

    arrived("stale")

    @pl.loop(0, HEADS // 2)
    def _(i):
        at = pl.multiple_of(i * 128, 128)
        keys = side_by_side(stale[:, pl.ds(at, 128)].astype(F32))
        vals = stale[:, pl.ds(pl.multiple_of(CHANS + i * 128, 128), 128)].astype(F32).T
        for sub in range(2):
            h = 2 * i + sub
            kvp[h, 0:COLS] = keys[sub].astype(BF16)
            for blk in range(4):
                kvp[h, COLS + blk * HEAD_DIM : COLS + (blk + 1) * HEAD_DIM] = vals[
                    sub * HEAD_DIM : (sub + 1) * HEAD_DIM, blk * 128 : (blk + 1) * 128
                ].astype(BF16)

    def to_owners(src, dst, send, recv, local):
        def far(h):
            return remote(src.at[h], dst.at[me], send.at[h], recv.at[me], owner(h))

        def near(h):
            return pltpu.make_async_copy(src.at[h], dst.at[me], local)

        def send_to(i):
            to = lax.rem(me + i, BANDS)
            head, found = jnp.int32(0), jnp.int32(0)
            for h in range(HEADS):
                hit = jnp.where(owner(h) == to, 1, 0)
                head, found = head + h * hit, found + hit

            @pl.when(found == 1)
            def _():
                remote(src.at[head], dst.at[me], send.at[head], recv.at[me], to).start()

        def start_column():
            for i in (4, 8, 12):
                send_to(i)
            for h in range(HEADS):
                @pl.when(owner(h) == me)
                def _():
                    near(h).start()

        def start_rest():
            @pl.loop(1, BANDS)
            def _(i):
                @pl.when(lax.rem(i, 4) != 0)
                def _():
                    send_to(i)

        def wait():
            for h in range(HEADS):
                @pl.when(owner(h) != me)
                def _():
                    far(h).wait_send()

                @pl.when(owner(h) == me)
                def _():
                    near(h).wait()

                    @pl.loop(1, BANDS)
                    def _(i):
                        frm = lax.rem(me + i, BANDS)
                        remote(src.at[h], dst.at[frm], send.at[h], recv.at[frm], frm).wait_recv()

        return start_column, start_rest, wait

    column_kv, rest_kv, wait_kv = to_owners(kvp, kv_all, kv_send, kv_recv, local_sem.at[6])
    column_q, rest_q, wait_q = to_owners(qp, q_all, q_send, q_recv, local_sem.at[7])

    column_kv()

    arrived("time")
    half = wfirst.shape[0] // 2
    lane = lanes((8, 2 * half))
    k = jnp.where(lane < half, lane, lane - half).astype(F32)
    angles = time_ref[0].astype(F32) * jnp.exp(-math.log(10000.0) * k / half)
    sinus = jnp.where(lane < half, jnp.cos(angles), jnp.sin(angles)).astype(BF16)
    hidden = jnp.dot(sinus, wfirst[...], preferred_element_type=F32)
    hidden = (hidden / (1.0 + jnp.exp(-hidden))).astype(BF16)
    tvec = jnp.dot(hidden, wsecond[...], preferred_element_type=F32)[0:1, :]

    arrived("gmat")
    wait_stats(0)
    mean, scale = merge_stats(stats_in.at[0], counts_ref, gain1_ref[...].astype(F32)[None], gmat[...])
    x_ref[0:COLS] = norm(latent_ref[0].astype(F32), mean, scale).astype(BF16)
    x_ref[COLS:TOK] = jnp.where(two, norm(latent_ref[1].astype(F32), mean, scale), 0.0).astype(BF16)

    arrived("conv")
    chunk = 256
    whole = 3 * CHANS // chunk

    def each_chunk(step):
        @pl.loop(0, whole)
        def _(i):
            step(pl.ds(pl.multiple_of(i * chunk, chunk), chunk))

        step(slice(whole * chunk, 3 * CHANS))

    def own_rows(at):
        mid = jnp.dot(x_ref[...], wcat[CHANS : 2 * CHANS, at], preferred_element_type=F32)
        under = jnp.dot(x_ref[COLS:TOK], wcat[2 * CHANS :, at], preferred_element_type=F32)
        over = jnp.dot(x_ref[0:COLS], wcat[0:CHANS, at], preferred_element_type=F32)
        y_ref[0:COLS, at] = mid[0:COLS] + under
        y_ref[COLS:TOK, at] = mid[COLS:TOK] + over

    each_chunk(own_rows)
    for c in halos:
        c.wait()
    rest_kv()
    x_ref[0:COLS] = jnp.where(
        jnp.full((COLS, CHANS), me, jnp.int32) > 0, norm(halo_in[0].astype(F32), mean, scale), 0.0
    ).astype(BF16)
    x_ref[COLS:TOK] = jnp.where(
        jnp.full((COLS, CHANS), me, jnp.int32) < BANDS - 1, norm(halo_in[1].astype(F32), mean, scale), 0.0
    ).astype(BF16)

    def other_rows(at):
        over = jnp.dot(x_ref[0:COLS], wcat[0:CHANS, at], preferred_element_type=F32)
        under = jnp.dot(x_ref[COLS:TOK], wcat[2 * CHANS :, at], preferred_element_type=F32)
        both = jnp.full(under.shape, mine, jnp.int32) == 2
        y_ref[0:COLS, at] = y_ref[0:COLS, at] + over + jnp.where(both, 0.0, under)
        y_ref[COLS:TOK, at] = y_ref[COLS:TOK, at] + jnp.where(both, under, 0.0)

    each_chunk(other_rows)
    row = lax.broadcasted_iota(jnp.int32, (COLS, CHANS), 0)
    for r in range(2):
        here = slice(r * COLS, (r + 1) * COLS)
        left = pltpu.roll(y_ref[here, 0:CHANS], 1, 0)
        right = pltpu.roll(y_ref[here, 2 * CHANS :], COLS - 1, 0)
        conv = y_ref[here, CHANS : 2 * CHANS] + jnp.where(row == 0, 0.0, left) + jnp.where(
            row == COLS - 1, 0.0, right
        )
        resid_ref[here, :] = (latent_ref[r].astype(F32) + conv + tvec).astype(BF16)

    local_stats(resid_ref[0:COLS].astype(F32), resid_ref[COLS:TOK].astype(F32), live1, stats_out.at[1])
    stats_in[1, me] = stats_out[1]
    send_stats(1)
    arrived("in")
    wait_stats(1)
    mean, scale = merge_stats(stats_in.at[1], counts_ref, gain2_ref[...].astype(F32)[None], gmat[...])
    x_ref[0:COLS] = norm(resid_ref[0:COLS].astype(F32), mean, scale).astype(BF16)
    x_ref[COLS:TOK] = jnp.where(two, norm(resid_ref[COLS:TOK].astype(F32), mean, scale), 0.0).astype(BF16)

    fold = HEAD_DIM**-0.5 * math.log2(math.e)
    query = jnp.dot(x_ref[...], win[:, 0:CHANS], preferred_element_type=F32) * fold
    low = lanes((TOK, 128)) < HEAD_DIM
    for i in range(HEADS // 2):
        pair = query[:, i * 128 : (i + 1) * 128]
        qs[2 * i] = jnp.where(low, pair, 0.0).astype(BF16)
        qs[2 * i + 1] = jnp.where(low, 0.0, pair).astype(BF16)
        for sub, packed in enumerate(side_by_side(pair)):
            qp[2 * i + sub] = packed.astype(BF16)
    rest_q()
    column_q()

    kf[...] = jnp.dot(x_ref[...], win[:, CHANS : 2 * CHANS], preferred_element_type=F32).astype(BF16)
    vals = jnp.dot(x_ref[...], win[:, 2 * CHANS :], preferred_element_type=F32)
    for i in range(HEADS // 2):
        vt[i * 128 : (i + 1) * 128] = vals[:, i * 128 : (i + 1) * 128].T.astype(BF16)
    shut = jnp.where(mine == 2, 0.0, NEG)
    ones = jnp.ones((16, TOK), BF16)

    @pl.loop(0, HEADS // 2)
    def _(i):
        keys = kf[:, pl.ds(pl.multiple_of(i * 128, 128), 128)]
        for sub in range(2):
            h = 2 * i + sub
            chans = pl.ds(pl.multiple_of(h * HEAD_DIM, HEAD_DIM), HEAD_DIM)
            values = jnp.concatenate([vt[chans], ones], axis=0)
            for r in range(2):
                here = slice(r * COLS, (r + 1) * COLS)
                s = lax.dot_general(
                    keys, qs[h, here], (((1,), (1,)), ((), ())), preferred_element_type=F32
                )
                s0, s1 = s[0:COLS], s[COLS:TOK] + shut
                best = jnp.max(jnp.maximum(s0, s1), axis=0, keepdims=True)
                w = jnp.concatenate([jnp.exp2(s0 - best), jnp.exp2(s1 - best)], axis=0).astype(BF16)
                acc = jnp.dot(values, w, preferred_element_type=F32)
                total = acc[HEAD_DIM : HEAD_DIM + 1]
                own_ref[chans, here] = (acc[0:HEAD_DIM] / total).astype(BF16)
                lse_ref[h, r : r + 1, :] = best + jnp.log2(total)

    wait_kv()
    wait_q()


STEP = 4
AHEAD = 4
LIST = 24


def attend(
    counts_ref, window_ref, q_hbm, kv_hbm, o_ref, lse_ref,
    q_ref, kv_ref, local_sem, keys_list, step_q, step_k, step_left, step_flag, kx, qx, vx, s_ref, top_ref, best_ref, acc_ref,
):
    me = lax.axis_index("patch")
    mine = owner(0) == me
    for h in range(1, HEADS):
        mine = jnp.logical_or(mine, owner(h) == me)
    low = lanes((COLS, 128)) < HEAD_DIM

    def unpack(j):
        ones = jnp.ones((16, COLS), BF16)

        def values(r):
            at = COLS + 2 * r * HEAD_DIM
            pair = [kv_ref[j, at : at + HEAD_DIM], kv_ref[j, at + HEAD_DIM : at + 2 * HEAD_DIM]]
            return jnp.concatenate([jnp.concatenate(pair, axis=1), ones], axis=0)

        keys, q = kv_ref[j, 0:COLS], q_ref[j]
        kx[2 * j] = keys
        qx[2 * j] = jnp.where(low, q, jnp.zeros_like(q))
        vx[2 * j] = values(0)

        @pl.when(counts_ref[j] == 2)
        def _():
            kx[2 * j + 1] = swap(keys.astype(F32)).astype(BF16)
            qx[2 * j + 1] = jnp.where(low, swap(q.astype(F32)), 0.0).astype(BF16)
            vx[2 * j + 1] = values(1)

    def plan(p, t):
        base = p * LIST
        end = base
        for j in range(BANDS):
            seen = jnp.where(jnp.logical_and(window_ref[p, j] == 1, p != j), 1, 0)
            keys_list[end] = 2 * j
            end = end + seen
            keys_list[end] = 2 * j + 1
            end = end + seen * (counts_ref[j] - 1)
        for u in range(STEP - 1):
            keys_list[end + u] = 0
        n = end - base
        chunks = (n + STEP - 1) // STEP

        def row(r, t):
            def chunk(c, t):
                step_q[t] = 2 * p + r
                step_k[t] = base + STEP * c
                step_left[t] = n - STEP * c
                step_flag[t] = jnp.where(c == 0, 1, 0) + jnp.where(c == chunks - 1, 2, 0)
                return t + 1

            return lax.fori_loop(0, chunks, chunk, t)

        return lax.fori_loop(0, counts_ref[p], row, t)

    def score(t, slot, u):
        s = lax.dot_general(
            kx[keys_list[step_k[t] + u]], qx[step_q[t]], (((1,), (1,)), ((), ())), preferred_element_type=F32
        )
        if u > 0:
            s = s + jnp.where(u < step_left[t], 0.0, NEG)
        s_ref[slot, u * COLS : (u + 1) * COLS] = s
        return jnp.max(s.reshape(COLS // 8, 8, COLS), axis=0)

    def keep_top(slot, tops):
        top = tops[0]
        for other in tops[1:]:
            top = jnp.maximum(top, other)
        top_ref[slot] = jnp.max(top, axis=0, keepdims=True)

    def scores(t, slot):
        keep_top(slot, [score(t, slot, u) for u in range(STEP)])

    def weigh(t, slot, later, later_slot):
        flag = step_flag[t]
        fresh = lax.rem(flag, 2) == 1
        old = jnp.where(fresh, NEG, best_ref[...])
        best = jnp.maximum(old, top_ref[slot])
        best_ref[...] = best
        acc = acc_ref[...] * jnp.where(fresh, 0.0, jnp.exp2(old - best))
        tops = []
        for u in range(STEP):
            w = jnp.exp2(s_ref[slot, u * COLS : (u + 1) * COLS] - best).astype(BF16)
            tops.append(score(later, later_slot, u))
            acc = acc + jnp.dot(vx[keys_list[step_k[t] + u]], w, preferred_element_type=F32)
        acc_ref[...] = acc
        keep_top(later_slot, tops)
        return acc, best, flag, step_q[t]

    def finish(acc, best, flag, qi):
        @pl.when(flag >= 2)
        def _():
            p, r = qi // 2, lax.rem(qi, 2)
            total = acc[HEAD_DIM : HEAD_DIM + 1]
            here = pl.ds(pl.multiple_of(r * HEAD_DIM, HEAD_DIM), HEAD_DIM)
            o_ref[p, here] = (acc[0:HEAD_DIM] / total).astype(BF16)
            lse_ref[p, pl.ds(r, 1)] = best + jnp.log2(total)

    @pl.when(mine)
    def _():
        copies = (
            pltpu.make_async_copy(q_hbm, q_ref, local_sem.at[0]),
            pltpu.make_async_copy(kv_hbm, kv_ref, local_sem.at[1]),
        )
        for c in copies:
            c.start()
        o_ref[...] = jnp.zeros_like(o_ref)
        lse_ref[...] = jnp.full(lse_ref.shape, NEG, F32)
        acc_ref[...] = jnp.zeros_like(acc_ref)
        best_ref[...] = jnp.full(best_ref.shape, NEG, F32)

        steps = lax.fori_loop(0, BANDS, plan, jnp.int32(0))
        for u in range(4 * AHEAD):
            step_q[steps + u] = 0
            step_k[steps + u] = 0
            step_left[steps + u] = 0
            step_flag[steps + u] = 0

        for c in copies:
            c.wait()

        @pl.loop(0, BANDS)
        def _(j):
            unpack(j)

        @pl.when(steps > 0)
        def _():
            for g in range(AHEAD):
                scores(g, g)

            @pl.loop(0, (steps + 2 * AHEAD - 1) // (2 * AHEAD))
            def _(i):
                for half in range(2):
                    now, then = half * AHEAD, (1 - half) * AHEAD
                    t = 2 * AHEAD * i + now
                    done = [weigh(t + g, now + g, t + AHEAD + g, then + g) for g in range(AHEAD)]
                    for d in done:
                        finish(*d)


def tail(
    counts_ref, o_hbm, lse_hbm, resid_hbm, own_hbm, own_lse_hbm, out_hbm, mixed_ref,
    wout, o_in, lse_in, resid, own, own_lse_ref, att, sums,
    local_sem, o_send, o_recv, l_send, l_recv,
):
    me = lax.axis_index("patch")
    barrier = meet(me)
    copies = [
        pltpu.make_async_copy(s, d, local_sem.at[0])
        for s, d in ((out_hbm, wout), (resid_hbm, resid), (own_hbm, own), (own_lse_hbm, own_lse_ref))
    ]
    for c in copies:
        c.start()
    pl.semaphore_wait(barrier, BANDS - 1)

    def heads_home(h):
        def far(i):
            to = lax.rem(me + i, BANDS)
            return (
                remote(o_hbm.at[to], o_in.at[h], o_send.at[to], o_recv.at[h], to),
                remote(lse_hbm.at[to], lse_in.at[h], l_send.at[to], l_recv.at[h], to),
            )

        def near():
            return (
                pltpu.make_async_copy(o_hbm.at[me], o_in.at[h], local_sem.at[1]),
                pltpu.make_async_copy(lse_hbm.at[me], lse_in.at[h], local_sem.at[1]),
            )

        return far, near

    for h in range(HEADS):
        @pl.when(owner(h) == me)
        def _():
            far, near = heads_home(h)

            @pl.loop(1, BANDS)
            def _(i):
                for c in far(i):
                    c.start()

            for c in near():
                c.start()

    for c in copies:
        c.wait()

    def arrived(h):
        @pl.when(owner(h) != me)
        def _():
            frm = owner(h)
            remote(o_hbm.at[0], o_in.at[h], o_send.at[0], o_recv.at[h], frm).wait_recv()
            remote(lse_hbm.at[0], lse_in.at[h], l_send.at[0], l_recv.at[h], frm).wait_recv()

        @pl.when(owner(h) == me)
        def _():
            for c in heads_home(h)[1]():
                c.wait()

    for first, last in ((0, 4), (4, 8), (8, HEADS)):
        for h in range(first, last):
            arrived(h)
        for h in range(first, last):
            chans = slice(h * HEAD_DIM, (h + 1) * HEAD_DIM)
            share = 1.0 / (1.0 + jnp.exp2(own_lse_ref[h] - lse_in[h]))
            for r in range(2):
                here = slice(r * COLS, (r + 1) * COLS)
                mine = own[chans, here].astype(F32)
                theirs = o_in[h, r * HEAD_DIM : (r + 1) * HEAD_DIM].astype(F32)
                att[chans, here] = (mine + (theirs - mine) * share[r : r + 1]).astype(BF16)
        chans = slice(first * HEAD_DIM, last * HEAD_DIM)
        for r in range(2):
            here = slice(r * COLS, (r + 1) * COLS)
            total = resid[here].astype(F32) if first == 0 else sums[here]
            total = total + lax.dot_general(
                att[chans, here], wout[chans], (((0,), (0,)), ((), ())), preferred_element_type=F32
            )
            if last < HEADS:
                sums[here] = total
                continue
            if r == 1:
                total = jnp.where(jnp.full(total.shape, counts_ref[me], jnp.int32) == 2, total, 0.0)
            mixed_ref[r] = total.astype(BF16)

    for h in range(HEADS):
        @pl.when(owner(h) == me)
        def _():
            far = heads_home(h)[0]

            @pl.loop(1, BANDS)
            def _(i):
                for c in far(i):
                    c.wait_send()


def body(
    latent, stale_kv, row_counts, window, time_index, norm_gain, conv_weight, time_first, time_second, attn_gain,
    attn_in, attn_out,
):
    smem = pl.BlockSpec(memory_space=pltpu.SMEM)
    vmem = pl.BlockSpec(memory_space=pltpu.VMEM)
    hbm = pl.BlockSpec(memory_space=pl.ANY)
    dma = pltpu.SemaphoreType.DMA
    shape = jax.ShapeDtypeStruct
    group = np.arange(CHANS) // (CHANS // GROUPS)
    gmat = jnp.asarray(group[:, None] == group[None, :], BF16)
    kv_all, q_all, resid, own, own_lse = pl.pallas_call(
        lead,
        out_shape=(
            shape((BANDS, TOK, 128), BF16),
            shape((BANDS, COLS, 128), BF16),
            shape((TOK, CHANS), BF16),
            shape((CHANS, TOK), BF16),
            shape((HEADS, 2, COLS), F32),
        ),
        in_specs=[smem, smem] + [hbm] * 9,
        out_specs=(hbm, hbm, vmem, vmem, vmem),
        scratch_shapes=[
            pltpu.VMEM((2, COLS, CHANS), BF16),
            pltpu.VMEM((CHANS,), BF16),
            pltpu.VMEM((CHANS,), BF16),
            pltpu.VMEM((TOK, 2 * CHANS), BF16),
            pltpu.VMEM((3 * CHANS, 3 * CHANS), BF16),
            pltpu.VMEM(time_first.shape, BF16),
            pltpu.VMEM(time_second.shape, BF16),
            pltpu.VMEM((CHANS, 3 * CHANS), BF16),
            pltpu.VMEM((CHANS, CHANS), BF16),
            pltpu.VMEM((COLS, CHANS), BF16),
            pltpu.VMEM((2, COLS, CHANS), BF16),
            pltpu.VMEM((2, 2, CHANS), F32),
            pltpu.VMEM((2, BANDS, 2, CHANS), F32),
            pltpu.VMEM((TOK, CHANS), BF16),
            pltpu.VMEM((TOK, 3 * CHANS), F32),
            pltpu.VMEM((HEADS, TOK, 128), BF16),
            pltpu.VMEM((HEADS, COLS, 128), BF16),
            pltpu.VMEM((HEADS, TOK, 128), BF16),
            pltpu.VMEM((TOK, CHANS), BF16),
            pltpu.VMEM((CHANS, TOK), BF16),
            dma((9,)),
            dma((2, BANDS)),
            dma((2, BANDS)),
            dma((2,)),
            dma((2,)),
            dma((HEADS,)),
            dma((BANDS,)),
            dma((HEADS,)),
            dma((BANDS,)),
        ],
        compiler_params=pltpu.CompilerParams(
            collective_id=0, has_side_effects=True, vmem_limit_bytes=56 << 20
        ),
        name="lead",
    )(
        row_counts, time_index, latent, norm_gain, attn_gain, stale_kv,
        conv_weight, time_first, time_second, attn_in, gmat,
    )
    number = pltpu.SMEM((256,), jnp.int32)
    o_all, lse_all = pl.pallas_call(
        attend,
        out_shape=(shape((BANDS, 2 * HEAD_DIM, COLS), BF16), shape((BANDS, 2, COLS), F32)),
        in_specs=[smem, smem, hbm, hbm],
        out_specs=(vmem, vmem),
        scratch_shapes=[
            pltpu.VMEM((BANDS, COLS, 128), BF16),
            pltpu.VMEM((BANDS, TOK, 128), BF16),
            dma((2,)),
            pltpu.SMEM((BANDS * LIST + 8,), jnp.int32),
            number,
            number,
            number,
            number,
            pltpu.VMEM((2 * BANDS, COLS, 128), BF16),
            pltpu.VMEM((2 * BANDS, COLS, 128), BF16),
            pltpu.VMEM((2 * BANDS, HEAD_DIM + 16, COLS), BF16),
            pltpu.VMEM((2 * AHEAD, STEP * COLS, COLS), F32),
            pltpu.VMEM((2 * AHEAD, 1, COLS), F32),
            pltpu.VMEM((1, COLS), F32),
            pltpu.VMEM((HEAD_DIM + 16, COLS), F32),
        ],
        compiler_params=pltpu.CompilerParams(vmem_limit_bytes=56 << 20),
        name="attend",
    )(row_counts, window, q_all, kv_all)
    return pl.pallas_call(
        tail,
        out_shape=shape((2, COLS, CHANS), BF16),
        in_specs=[smem] + [hbm] * 6,
        out_specs=vmem,
        scratch_shapes=[
            pltpu.VMEM((CHANS, CHANS), BF16),
            pltpu.VMEM((HEADS, 2 * HEAD_DIM, COLS), BF16),
            pltpu.VMEM((HEADS, 2, COLS), F32),
            pltpu.VMEM((TOK, CHANS), BF16),
            pltpu.VMEM((CHANS, TOK), BF16),
            pltpu.VMEM((HEADS, 2, COLS), F32),
            pltpu.VMEM((CHANS, TOK), BF16),
            pltpu.VMEM((TOK, CHANS), F32),
            dma((2,)),
            dma((BANDS,)),
            dma((HEADS,)),
            dma((BANDS,)),
            dma((HEADS,)),
        ],
        compiler_params=pltpu.CompilerParams(
            collective_id=1, has_side_effects=True, vmem_limit_bytes=56 << 20
        ),
        name="tail",
    )(row_counts, o_all, lse_all, resid, own, own_lse, attn_out)


def solution(mesh):
    part = P(("batch", "patch"))
    placed = (part, part, P("batch"), P("batch"), P("batch")) + (P(),) * 7
    return jax.shard_map(body, mesh=mesh, in_specs=placed, out_specs=part, check_vma=False)
```

```python
import math

import jax
import jax.numpy as jnp
import numpy as np
from jax import lax
from jax.experimental import pallas as pl
from jax.experimental.pallas import tpu as pltpu
from jax.sharding import PartitionSpec as P

HEAD_DIM = 64
GROUPS = 32
HEADS = 10
BANDS = 16
COLS = 256
CHANS = 640
TOK = 512
EPS = 1e-05
NEG = -1e30
MESH = pl.DeviceIdType.MESH
F32, BF16 = jnp.float32, jnp.bfloat16

OWNERS = ((0, 5, 10, 15, 1, 4, 11, 14, 3, 12), (0, 5, 10, 15, 2, 7, 8, 13, 6, 9))


def owner(head):
    core = lax.rem(lax.axis_index("batch"), 2)
    return OWNERS[0][head] + core * (OWNERS[1][head] - OWNERS[0][head])


def meet(me):
    barrier = pltpu.get_barrier_semaphore()

    @pl.loop(1, BANDS)
    def _(i):
        pl.semaphore_signal(
            barrier, inc=1, device_id={"patch": lax.rem(me + i, BANDS)}, device_id_type=MESH
        )

    return barrier


def remote(src, dst, send, recv, to):
    return pltpu.make_async_remote_copy(
        src, dst, send, recv, device_id={"patch": to}, device_id_type=MESH
    )


def lanes(shape):
    return lax.broadcasted_iota(jnp.int32, shape, 1)


def swap(x):
    return pltpu.roll(x, HEAD_DIM, 1)


def group_sum(vec, gmat):
    hi = vec.astype(BF16)
    rest = vec - hi.astype(F32)
    mid = rest.astype(BF16)
    low = (rest - mid.astype(F32)).astype(BF16)
    row = lax.broadcasted_iota(jnp.int32, (16, CHANS), 0)
    stack = jnp.where(
        row == 0,
        hi.astype(F32),
        jnp.where(row == 1, mid.astype(F32), jnp.where(row == 2, low.astype(F32), 0.0)),
    ).astype(BF16)
    out = jnp.dot(stack, gmat, preferred_element_type=F32)
    return jnp.sum(out, axis=0, keepdims=True)


def local_stats(x0, x1, live1, out_ref):
    tok = COLS * (1.0 + live1)
    sums = jnp.sum(x0, axis=0, keepdims=True) + live1 * jnp.sum(x1, axis=0, keepdims=True)
    mean = sums / tok
    d0, d1 = x0 - mean, x1 - mean
    spread = jnp.sum(d0 * d0, axis=0, keepdims=True) + live1 * jnp.sum(d1 * d1, axis=0, keepdims=True)
    out_ref[0:1, :] = sums
    out_ref[1:2, :] = spread


def merge_stats(stats_ref, counts_ref, gain, gmat):
    total = jnp.zeros((1, CHANS), F32)
    rows = 0
    for b in range(BANDS):
        total = total + stats_ref[b, 0:1, :]
        rows = rows + counts_ref[b]
    count = rows.astype(F32) * (COLS * (CHANS // GROUPS))
    mean = group_sum(total, gmat) / count
    spread = jnp.zeros((1, CHANS), F32)
    for b in range(BANDS):
        tok = counts_ref[b].astype(F32) * COLS
        off = stats_ref[b, 0:1, :] / tok - mean
        spread = spread + stats_ref[b, 1:2, :] + tok * (off * off)
    var = group_sum(spread, gmat) / count
    return mean, 0.5 * lax.rsqrt(var + EPS) * gain


def norm(x, mean, half):
    y = (x - mean) * half
    return y + y * jnp.tanh(y)


def side_by_side(x):
    turned = swap(x)
    low = lanes((COLS, 128)) < HEAD_DIM
    return jnp.where(low, x[0:COLS], turned[COLS:TOK]), jnp.where(low, turned[0:COLS], x[COLS:TOK])


def lead(
    counts_ref, time_ref, latent_hbm, gain1_hbm, gain2_hbm, stale_hbm, conv_hbm, first_hbm, second_hbm, in_hbm, gmat_hbm,
    kv_all, q_all, resid_ref, own_ref, lse_ref,
    latent_ref, gain1_ref, gain2_ref, stale, wcat, wfirst, wsecond, win, gmat, halo_out, halo_in, stats_out, stats_in, x_ref, y_ref,
    kvp, qp, qs, kf, vt,
    local_sem, stat_send, stat_recv, halo_send, halo_recv, kv_send, kv_recv, q_send, q_recv,
):
    me = lax.axis_index("patch")
    up, down = lax.rem(me + 1, BANDS), lax.rem(me + BANDS - 1, BANDS)
    barrier = meet(me)

    copies = {
        "latent": [(latent_hbm, latent_ref)],
        "stale": [(stale_hbm, stale)],
        "gmat": [(gmat_hbm, gmat), (gain1_hbm, gain1_ref), (gain2_hbm, gain2_ref)],
        "time": [(first_hbm, wfirst), (second_hbm, wsecond)],
        "conv": [
            (conv_hbm.at[dy, dx], wcat.at[pl.ds(dy * CHANS, CHANS), pl.ds(dx * CHANS, CHANS)])
            for dy in range(3)
            for dx in range(3)
        ],
        "in": [(in_hbm, win)],
    }
    copies = {
        name: [pltpu.make_async_copy(s, d, local_sem.at[i]) for s, d in pairs]
        for i, (name, pairs) in enumerate(copies.items())
    }
    for group in copies.values():
        for c in group:
            c.start()

    def arrived(name):
        for c in copies[name]:
            c.wait()

    mine = counts_ref[me]
    live1 = (mine - 1).astype(F32)
    two = jnp.full((COLS, CHANS), mine, jnp.int32) == 2

    arrived("latent")
    halo_out[...] = jnp.where(two, latent_ref[1], latent_ref[0])
    local_stats(latent_ref[0].astype(F32), latent_ref[1].astype(F32), live1, stats_out.at[0])
    stats_in[0, me] = stats_out[0]

    pl.semaphore_wait(barrier, BANDS - 1)

    def send_stats(turn):
        @pl.loop(1, BANDS)
        def _(i):
            to = lax.rem(me + i, BANDS)
            remote(
                stats_out.at[turn], stats_in.at[turn, me], stat_send.at[turn, to], stat_recv.at[turn, me], to
            ).start()

    def wait_stats(turn):
        @pl.loop(1, BANDS)
        def _(i):
            to = lax.rem(me + i, BANDS)
            c = remote(
                stats_out.at[turn], stats_in.at[turn, to], stat_send.at[turn, to], stat_recv.at[turn, to], to
            )
            c.wait_send()
            c.wait_recv()

    halos = (
        remote(halo_out, halo_in.at[0], halo_send.at[0], halo_recv.at[0], up),
        remote(latent_ref.at[0], halo_in.at[1], halo_send.at[1], halo_recv.at[1], down),
    )
    send_stats(0)
    for c in halos:
        c.start()

    arrived("stale")

    @pl.loop(0, HEADS // 2)
    def _(i):
        at = pl.multiple_of(i * 128, 128)
        keys = side_by_side(stale[:, pl.ds(at, 128)].astype(F32))
        vals = stale[:, pl.ds(pl.multiple_of(CHANS + i * 128, 128), 128)].astype(F32).T
        for sub in range(2):
            h = 2 * i + sub
            kvp[h, 0:COLS] = keys[sub].astype(BF16)
            for blk in range(4):
                kvp[h, COLS + blk * HEAD_DIM : COLS + (blk + 1) * HEAD_DIM] = vals[
                    sub * HEAD_DIM : (sub + 1) * HEAD_DIM, blk * 128 : (blk + 1) * 128
                ].astype(BF16)

    def to_owners(src, dst, send, recv, local):
        def far(h):
            return remote(src.at[h], dst.at[me], send.at[h], recv.at[me], owner(h))

        def near(h):
            return pltpu.make_async_copy(src.at[h], dst.at[me], local)

        def send_to(i):
            to = lax.rem(me + i, BANDS)
            head, found = jnp.int32(0), jnp.int32(0)
            for h in range(HEADS):
                hit = jnp.where(owner(h) == to, 1, 0)
                head, found = head + h * hit, found + hit

            @pl.when(found == 1)
            def _():
                remote(src.at[head], dst.at[me], send.at[head], recv.at[me], to).start()

        def start_column():
            for i in (4, 8, 12):
                send_to(i)
            for h in range(HEADS):
                @pl.when(owner(h) == me)
                def _():
                    near(h).start()

        def start_rest():
            @pl.loop(1, BANDS)
            def _(i):
                @pl.when(lax.rem(i, 4) != 0)
                def _():
                    send_to(i)

        def wait():
            for h in range(HEADS):
                @pl.when(owner(h) != me)
                def _():
                    far(h).wait_send()

                @pl.when(owner(h) == me)
                def _():
                    near(h).wait()

                    @pl.loop(1, BANDS)
                    def _(i):
                        frm = lax.rem(me + i, BANDS)
                        remote(src.at[h], dst.at[frm], send.at[h], recv.at[frm], frm).wait_recv()

        return start_column, start_rest, wait

    column_kv, rest_kv, wait_kv = to_owners(kvp, kv_all, kv_send, kv_recv, local_sem.at[6])
    column_q, rest_q, wait_q = to_owners(qp, q_all, q_send, q_recv, local_sem.at[7])

    column_kv()

    arrived("time")
    half = wfirst.shape[0] // 2
    lane = lanes((8, 2 * half))
    k = jnp.where(lane < half, lane, lane - half).astype(F32)
    angles = time_ref[0].astype(F32) * jnp.exp(-math.log(10000.0) * k / half)
    sinus = jnp.where(lane < half, jnp.cos(angles), jnp.sin(angles)).astype(BF16)
    hidden = jnp.dot(sinus, wfirst[...], preferred_element_type=F32)
    hidden = (hidden / (1.0 + jnp.exp(-hidden))).astype(BF16)
    tvec = jnp.dot(hidden, wsecond[...], preferred_element_type=F32)[0:1, :]

    arrived("gmat")
    wait_stats(0)
    mean, scale = merge_stats(stats_in.at[0], counts_ref, gain1_ref[...].astype(F32)[None], gmat[...])
    x_ref[0:COLS] = norm(latent_ref[0].astype(F32), mean, scale).astype(BF16)
    x_ref[COLS:TOK] = jnp.where(two, norm(latent_ref[1].astype(F32), mean, scale), 0.0).astype(BF16)

    arrived("conv")
    chunk = 256
    whole = 3 * CHANS // chunk

    def each_chunk(step):
        @pl.loop(0, whole)
        def _(i):
            step(pl.ds(pl.multiple_of(i * chunk, chunk), chunk))

        step(slice(whole * chunk, 3 * CHANS))

    def own_rows(at):
        mid = jnp.dot(x_ref[...], wcat[CHANS : 2 * CHANS, at], preferred_element_type=F32)
        under = jnp.dot(x_ref[COLS:TOK], wcat[2 * CHANS :, at], preferred_element_type=F32)
        over = jnp.dot(x_ref[0:COLS], wcat[0:CHANS, at], preferred_element_type=F32)
        y_ref[0:COLS, at] = mid[0:COLS] + under
        y_ref[COLS:TOK, at] = mid[COLS:TOK] + over

    each_chunk(own_rows)
    for c in halos:
        c.wait()
    rest_kv()
    x_ref[0:COLS] = jnp.where(
        jnp.full((COLS, CHANS), me, jnp.int32) > 0, norm(halo_in[0].astype(F32), mean, scale), 0.0
    ).astype(BF16)
    x_ref[COLS:TOK] = jnp.where(
        jnp.full((COLS, CHANS), me, jnp.int32) < BANDS - 1, norm(halo_in[1].astype(F32), mean, scale), 0.0
    ).astype(BF16)

    def other_rows(at):
        over = jnp.dot(x_ref[0:COLS], wcat[0:CHANS, at], preferred_element_type=F32)
        under = jnp.dot(x_ref[COLS:TOK], wcat[2 * CHANS :, at], preferred_element_type=F32)
        both = jnp.full(under.shape, mine, jnp.int32) == 2
        y_ref[0:COLS, at] = y_ref[0:COLS, at] + over + jnp.where(both, 0.0, under)
        y_ref[COLS:TOK, at] = y_ref[COLS:TOK, at] + jnp.where(both, under, 0.0)

    each_chunk(other_rows)
    row = lax.broadcasted_iota(jnp.int32, (COLS, CHANS), 0)
    for r in range(2):
        here = slice(r * COLS, (r + 1) * COLS)
        left = pltpu.roll(y_ref[here, 0:CHANS], 1, 0)
        right = pltpu.roll(y_ref[here, 2 * CHANS :], COLS - 1, 0)
        conv = y_ref[here, CHANS : 2 * CHANS] + jnp.where(row == 0, 0.0, left) + jnp.where(
            row == COLS - 1, 0.0, right
        )
        resid_ref[here, :] = (latent_ref[r].astype(F32) + conv + tvec).astype(BF16)

    local_stats(resid_ref[0:COLS].astype(F32), resid_ref[COLS:TOK].astype(F32), live1, stats_out.at[1])
    stats_in[1, me] = stats_out[1]
    send_stats(1)
    arrived("in")
    wait_stats(1)
    mean, scale = merge_stats(stats_in.at[1], counts_ref, gain2_ref[...].astype(F32)[None], gmat[...])
    x_ref[0:COLS] = norm(resid_ref[0:COLS].astype(F32), mean, scale).astype(BF16)
    x_ref[COLS:TOK] = jnp.where(two, norm(resid_ref[COLS:TOK].astype(F32), mean, scale), 0.0).astype(BF16)

    fold = HEAD_DIM**-0.5 * math.log2(math.e)
    query = jnp.dot(x_ref[...], win[:, 0:CHANS], preferred_element_type=F32) * fold
    low = lanes((TOK, 128)) < HEAD_DIM
    for i in range(HEADS // 2):
        pair = query[:, i * 128 : (i + 1) * 128]
        qs[2 * i] = jnp.where(low, pair, 0.0).astype(BF16)
        qs[2 * i + 1] = jnp.where(low, 0.0, pair).astype(BF16)
        for sub, packed in enumerate(side_by_side(pair)):
            qp[2 * i + sub] = packed.astype(BF16)
    rest_q()
    column_q()

    kf[...] = jnp.dot(x_ref[...], win[:, CHANS : 2 * CHANS], preferred_element_type=F32).astype(BF16)
    vals = jnp.dot(x_ref[...], win[:, 2 * CHANS :], preferred_element_type=F32)
    for i in range(HEADS // 2):
        vt[i * 128 : (i + 1) * 128] = vals[:, i * 128 : (i + 1) * 128].T.astype(BF16)
    shut = jnp.where(mine == 2, 0.0, NEG)
    ones = jnp.ones((16, TOK), BF16)

    @pl.loop(0, HEADS // 2)
    def _(i):
        keys = kf[:, pl.ds(pl.multiple_of(i * 128, 128), 128)]
        for sub in range(2):
            h = 2 * i + sub
            chans = pl.ds(pl.multiple_of(h * HEAD_DIM, HEAD_DIM), HEAD_DIM)
            values = jnp.concatenate([vt[chans], ones], axis=0)
            for r in range(2):
                here = slice(r * COLS, (r + 1) * COLS)
                s = lax.dot_general(
                    keys, qs[h, here], (((1,), (1,)), ((), ())), preferred_element_type=F32
                )
                s0, s1 = s[0:COLS], s[COLS:TOK] + shut
                best = jnp.max(jnp.maximum(s0, s1), axis=0, keepdims=True)
                w = jnp.concatenate([jnp.exp2(s0 - best), jnp.exp2(s1 - best)], axis=0).astype(BF16)
                acc = jnp.dot(values, w, preferred_element_type=F32)
                total = acc[HEAD_DIM : HEAD_DIM + 1]
                own_ref[chans, here] = (acc[0:HEAD_DIM] / total).astype(BF16)
                lse_ref[h, r : r + 1, :] = best + jnp.log2(total)

    wait_kv()
    wait_q()


STEP = 4
AHEAD = 4
LIST = 24


def attend(
    counts_ref, window_ref, q_hbm, kv_hbm, o_ref, lse_ref,
    q_ref, kv_ref, local_sem, keys_list, step_q, step_k, step_left, step_flag, kx, qx, vx, s_ref, top_ref, best_ref, acc_ref,
):
    me = lax.axis_index("patch")
    mine = owner(0) == me
    for h in range(1, HEADS):
        mine = jnp.logical_or(mine, owner(h) == me)
    low = lanes((COLS, 128)) < HEAD_DIM

    def unpack(j):
        ones = jnp.ones((16, COLS), BF16)

        def values(r):
            at = COLS + 2 * r * HEAD_DIM
            pair = [kv_ref[j, at : at + HEAD_DIM], kv_ref[j, at + HEAD_DIM : at + 2 * HEAD_DIM]]
            return jnp.concatenate([jnp.concatenate(pair, axis=1), ones], axis=0)

        keys, q = kv_ref[j, 0:COLS], q_ref[j]
        kx[2 * j] = keys
        qx[2 * j] = jnp.where(low, q, jnp.zeros_like(q))
        vx[2 * j] = values(0)

        @pl.when(counts_ref[j] == 2)
        def _():
            kx[2 * j + 1] = swap(keys.astype(F32)).astype(BF16)
            qx[2 * j + 1] = jnp.where(low, swap(q.astype(F32)), 0.0).astype(BF16)
            vx[2 * j + 1] = values(1)

    def plan(p, t):
        base = p * LIST
        end = base
        for j in range(BANDS):
            seen = jnp.where(jnp.logical_and(window_ref[p, j] == 1, p != j), 1, 0)
            keys_list[end] = 2 * j
            end = end + seen
            keys_list[end] = 2 * j + 1
            end = end + seen * (counts_ref[j] - 1)
        for u in range(STEP - 1):
            keys_list[end + u] = 0
        n = end - base
        chunks = (n + STEP - 1) // STEP

        def row(r, t):
            def chunk(c, t):
                step_q[t] = 2 * p + r
                step_k[t] = base + STEP * c
                step_left[t] = n - STEP * c
                step_flag[t] = jnp.where(c == 0, 1, 0) + jnp.where(c == chunks - 1, 2, 0)
                return t + 1

            return lax.fori_loop(0, chunks, chunk, t)

        return lax.fori_loop(0, counts_ref[p], row, t)

    def score(t, slot, u):
        s = lax.dot_general(
            kx[keys_list[step_k[t] + u]], qx[step_q[t]], (((1,), (1,)), ((), ())), preferred_element_type=F32
        )
        if u > 0:
            s = s + jnp.where(u < step_left[t], 0.0, NEG)
        s_ref[slot, u * COLS : (u + 1) * COLS] = s
        return jnp.max(s.reshape(COLS // 8, 8, COLS), axis=0)

    def keep_top(slot, tops):
        top = tops[0]
        for other in tops[1:]:
            top = jnp.maximum(top, other)
        top_ref[slot] = jnp.max(top, axis=0, keepdims=True)

    def scores(t, slot):
        keep_top(slot, [score(t, slot, u) for u in range(STEP)])

    def weigh(t, slot, later, later_slot):
        flag = step_flag[t]
        fresh = lax.rem(flag, 2) == 1
        old = jnp.where(fresh, NEG, best_ref[...])
        best = jnp.maximum(old, top_ref[slot])
        best_ref[...] = best
        acc = acc_ref[...] * jnp.where(fresh, 0.0, jnp.exp2(old - best))
        tops = []
        for u in range(STEP):
            w = jnp.exp2(s_ref[slot, u * COLS : (u + 1) * COLS] - best).astype(BF16)
            tops.append(score(later, later_slot, u))
            acc = acc + jnp.dot(vx[keys_list[step_k[t] + u]], w, preferred_element_type=F32)
        acc_ref[...] = acc
        keep_top(later_slot, tops)
        return acc, best, flag, step_q[t]

    def finish(acc, best, flag, qi):
        @pl.when(flag >= 2)
        def _():
            p, r = qi // 2, lax.rem(qi, 2)
            total = acc[HEAD_DIM : HEAD_DIM + 1]
            here = pl.ds(pl.multiple_of(r * HEAD_DIM, HEAD_DIM), HEAD_DIM)
            o_ref[p, here] = (acc[0:HEAD_DIM] / total).astype(BF16)
            lse_ref[p, pl.ds(r, 1)] = best + jnp.log2(total)

    @pl.when(mine)
    def _():
        copies = (
            pltpu.make_async_copy(q_hbm, q_ref, local_sem.at[0]),
            pltpu.make_async_copy(kv_hbm, kv_ref, local_sem.at[1]),
        )
        for c in copies:
            c.start()
        o_ref[...] = jnp.zeros_like(o_ref)
        lse_ref[...] = jnp.full(lse_ref.shape, NEG, F32)
        acc_ref[...] = jnp.zeros_like(acc_ref)
        best_ref[...] = jnp.full(best_ref.shape, NEG, F32)

        for c in copies:
            c.wait()

        def prepare(p, t):
            unpack(p)
            return plan(p, t)

        steps = lax.fori_loop(0, BANDS, prepare, jnp.int32(0))
        for u in range(4 * AHEAD):
            step_q[steps + u] = 0
            step_k[steps + u] = 0
            step_left[steps + u] = 0
            step_flag[steps + u] = 0

        @pl.when(steps > 0)
        def _():
            for g in range(AHEAD):
                scores(g, g)

            @pl.loop(0, (steps + 2 * AHEAD - 1) // (2 * AHEAD))
            def _(i):
                for half in range(2):
                    now, then = half * AHEAD, (1 - half) * AHEAD
                    t = 2 * AHEAD * i + now
                    done = [weigh(t + g, now + g, t + AHEAD + g, then + g) for g in range(AHEAD)]
                    for d in done:
                        finish(*d)


def tail(
    counts_ref, o_hbm, lse_hbm, resid_hbm, own_hbm, own_lse_hbm, out_hbm, mixed_ref,
    wout, o_in, lse_in, resid, own, own_lse_ref, att, sums,
    local_sem, o_send, o_recv, l_send, l_recv,
):
    me = lax.axis_index("patch")
    barrier = meet(me)
    copies = [
        pltpu.make_async_copy(s, d, local_sem.at[0])
        for s, d in ((out_hbm, wout), (resid_hbm, resid), (own_hbm, own), (own_lse_hbm, own_lse_ref))
    ]
    for c in copies:
        c.start()
    pl.semaphore_wait(barrier, BANDS - 1)

    def heads_home(h):
        def far(i):
            to = lax.rem(me + i, BANDS)
            return (
                remote(o_hbm.at[to], o_in.at[h], o_send.at[to], o_recv.at[h], to),
                remote(lse_hbm.at[to], lse_in.at[h], l_send.at[to], l_recv.at[h], to),
            )

        def near():
            return (
                pltpu.make_async_copy(o_hbm.at[me], o_in.at[h], local_sem.at[1]),
                pltpu.make_async_copy(lse_hbm.at[me], lse_in.at[h], local_sem.at[1]),
            )

        return far, near

    for h in range(HEADS):
        @pl.when(owner(h) == me)
        def _():
            far, near = heads_home(h)

            @pl.loop(1, BANDS)
            def _(i):
                for c in far(i):
                    c.start()

            for c in near():
                c.start()

    for c in copies:
        c.wait()

    def arrived(h):
        @pl.when(owner(h) != me)
        def _():
            frm = owner(h)
            remote(o_hbm.at[0], o_in.at[h], o_send.at[0], o_recv.at[h], frm).wait_recv()
            remote(lse_hbm.at[0], lse_in.at[h], l_send.at[0], l_recv.at[h], frm).wait_recv()

        @pl.when(owner(h) == me)
        def _():
            for c in heads_home(h)[1]():
                c.wait()

    for first, last in ((0, 4), (4, 8), (8, HEADS)):
        for h in range(first, last):
            arrived(h)
        for h in range(first, last):
            chans = slice(h * HEAD_DIM, (h + 1) * HEAD_DIM)
            share = 1.0 / (1.0 + jnp.exp2(own_lse_ref[h] - lse_in[h]))
            for r in range(2):
                here = slice(r * COLS, (r + 1) * COLS)
                mine = own[chans, here].astype(F32)
                theirs = o_in[h, r * HEAD_DIM : (r + 1) * HEAD_DIM].astype(F32)
                att[chans, here] = (mine + (theirs - mine) * share[r : r + 1]).astype(BF16)
        chans = slice(first * HEAD_DIM, last * HEAD_DIM)
        for r in range(2):
            here = slice(r * COLS, (r + 1) * COLS)
            total = resid[here].astype(F32) if first == 0 else sums[here]
            total = total + lax.dot_general(
                att[chans, here], wout[chans], (((0,), (0,)), ((), ())), preferred_element_type=F32
            )
            if last < HEADS:
                sums[here] = total
                continue
            if r == 1:
                total = jnp.where(jnp.full(total.shape, counts_ref[me], jnp.int32) == 2, total, 0.0)
            mixed_ref[r] = total.astype(BF16)

    for h in range(HEADS):
        @pl.when(owner(h) == me)
        def _():
            far = heads_home(h)[0]

            @pl.loop(1, BANDS)
            def _(i):
                for c in far(i):
                    c.wait_send()


def body(
    latent, stale_kv, row_counts, window, time_index, norm_gain, conv_weight, time_first, time_second, attn_gain,
    attn_in, attn_out,
):
    smem = pl.BlockSpec(memory_space=pltpu.SMEM)
    vmem = pl.BlockSpec(memory_space=pltpu.VMEM)
    hbm = pl.BlockSpec(memory_space=pl.ANY)
    dma = pltpu.SemaphoreType.DMA
    shape = jax.ShapeDtypeStruct
    group = np.arange(CHANS) // (CHANS // GROUPS)
    gmat = jnp.asarray(group[:, None] == group[None, :], BF16)
    kv_all, q_all, resid, own, own_lse = pl.pallas_call(
        lead,
        out_shape=(
            shape((BANDS, TOK, 128), BF16),
            shape((BANDS, COLS, 128), BF16),
            shape((TOK, CHANS), BF16),
            shape((CHANS, TOK), BF16),
            shape((HEADS, 2, COLS), F32),
        ),
        in_specs=[smem, smem] + [hbm] * 9,
        out_specs=(hbm, hbm, vmem, vmem, vmem),
        scratch_shapes=[
            pltpu.VMEM((2, COLS, CHANS), BF16),
            pltpu.VMEM((CHANS,), BF16),
            pltpu.VMEM((CHANS,), BF16),
            pltpu.VMEM((TOK, 2 * CHANS), BF16),
            pltpu.VMEM((3 * CHANS, 3 * CHANS), BF16),
            pltpu.VMEM(time_first.shape, BF16),
            pltpu.VMEM(time_second.shape, BF16),
            pltpu.VMEM((CHANS, 3 * CHANS), BF16),
            pltpu.VMEM((CHANS, CHANS), BF16),
            pltpu.VMEM((COLS, CHANS), BF16),
            pltpu.VMEM((2, COLS, CHANS), BF16),
            pltpu.VMEM((2, 2, CHANS), F32),
            pltpu.VMEM((2, BANDS, 2, CHANS), F32),
            pltpu.VMEM((TOK, CHANS), BF16),
            pltpu.VMEM((TOK, 3 * CHANS), F32),
            pltpu.VMEM((HEADS, TOK, 128), BF16),
            pltpu.VMEM((HEADS, COLS, 128), BF16),
            pltpu.VMEM((HEADS, TOK, 128), BF16),
            pltpu.VMEM((TOK, CHANS), BF16),
            pltpu.VMEM((CHANS, TOK), BF16),
            dma((9,)),
            dma((2, BANDS)),
            dma((2, BANDS)),
            dma((2,)),
            dma((2,)),
            dma((HEADS,)),
            dma((BANDS,)),
            dma((HEADS,)),
            dma((BANDS,)),
        ],
        compiler_params=pltpu.CompilerParams(
            collective_id=0, has_side_effects=True, vmem_limit_bytes=56 << 20
        ),
        name="lead",
    )(
        row_counts, time_index, latent, norm_gain, attn_gain, stale_kv,
        conv_weight, time_first, time_second, attn_in, gmat,
    )
    number = pltpu.SMEM((256,), jnp.int32)
    o_all, lse_all = pl.pallas_call(
        attend,
        out_shape=(shape((BANDS, 2 * HEAD_DIM, COLS), BF16), shape((BANDS, 2, COLS), F32)),
        in_specs=[smem, smem, hbm, hbm],
        out_specs=(vmem, vmem),
        scratch_shapes=[
            pltpu.VMEM((BANDS, COLS, 128), BF16),
            pltpu.VMEM((BANDS, TOK, 128), BF16),
            dma((2,)),
            pltpu.SMEM((BANDS * LIST + 8,), jnp.int32),
            number,
            number,
            number,
            number,
            pltpu.VMEM((2 * BANDS, COLS, 128), BF16),
            pltpu.VMEM((2 * BANDS, COLS, 128), BF16),
            pltpu.VMEM((2 * BANDS, HEAD_DIM + 16, COLS), BF16),
            pltpu.VMEM((2 * AHEAD, STEP * COLS, COLS), F32),
            pltpu.VMEM((2 * AHEAD, 1, COLS), F32),
            pltpu.VMEM((1, COLS), F32),
            pltpu.VMEM((HEAD_DIM + 16, COLS), F32),
        ],
        compiler_params=pltpu.CompilerParams(vmem_limit_bytes=56 << 20),
        name="attend",
    )(row_counts, window, q_all, kv_all)
    return pl.pallas_call(
        tail,
        out_shape=shape((2, COLS, CHANS), BF16),
        in_specs=[smem] + [hbm] * 6,
        out_specs=vmem,
        scratch_shapes=[
            pltpu.VMEM((CHANS, CHANS), BF16),
            pltpu.VMEM((HEADS, 2 * HEAD_DIM, COLS), BF16),
            pltpu.VMEM((HEADS, 2, COLS), F32),
            pltpu.VMEM((TOK, CHANS), BF16),
            pltpu.VMEM((CHANS, TOK), BF16),
            pltpu.VMEM((HEADS, 2, COLS), F32),
            pltpu.VMEM((CHANS, TOK), BF16),
            pltpu.VMEM((TOK, CHANS), F32),
            dma((2,)),
            dma((BANDS,)),
            dma((HEADS,)),
            dma((BANDS,)),
            dma((HEADS,)),
        ],
        compiler_params=pltpu.CompilerParams(
            collective_id=1, has_side_effects=True, vmem_limit_bytes=56 << 20
        ),
        name="tail",
    )(row_counts, o_all, lse_all, resid, own, own_lse, attn_out)


def solution(mesh):
    part = P(("batch", "patch"))
    placed = (part, part, P("batch"), P("batch"), P("batch")) + (P(),) * 7
    return jax.shard_map(body, mesh=mesh, in_specs=placed, out_specs=part, check_vma=False)
```
